32 devices in a mesh: section: 2 (over x), ctx: 16 (over z, y, core).
Axes of the slice: x: 2, y: 2, z: 4, core: 2. Of those that a mesh axis runs over, the one named last changes fastest.
Arguments:
- stream: bfloat16 [2, 3072, 8192], P('section', 'ctx'), may hold values from -1.5 to 1.5
- queries: bfloat16 [2, 3072, 8192], P('section', 'ctx'), may hold values from -24 to 24
- keys: bfloat16 [2, 3072, 1024], P('section', 'ctx'), may hold values from -24 to 24
- values: bfloat16 [2, 3072, 1024], P('section', 'ctx'), may hold values from -6 to 6
- segments: int32 [2, 3072], P('section', 'ctx'), may hold values from 0 to 7, never falling along the last dimension, each value on 1 to 1344 neighbouring positions
Outputs:
- next_stream: bfloat16 [2, 3072, 8192], P('section', 'ctx')
The draws below stay inside these ranges and needn't reach their ends.
Inputs may be any that keep to these rules, and one draw needn't show every extreme that they name: `segments`: along each micro-batch the numbers never fall; each document holds at most (7) * 192 tokens, and one holds exactly that many.
All inputs are finite; a program needn't handle non-finite values.
Results may differ from the reference program's by a relative error of at most 0.0095.
Values may be sent and summed in bfloat16 or wider, within the bound.
No kernel may reach another device: no remote copies, remote signals or barrier semaphores. Data moves between devices by JAX's collectives and lax.ppermute only.
A program may use at most 128 MiB of HBM per device.

```python
import math
import jax
import jax.numpy as jnp
import numpy as np
from jax import lax

HQ = 64
KVH = 8
HD = 128
TOK_DEV = 192
WINDOW = 8
D = 8192
MICRO = 2
SEQ = 3072
DOCS = 8


def draw_queries(key, part):
    repeat = HQ // KVH
    full = jnp.clip(jax.random.normal(jax.random.fold_in(key, 1), (MICRO, SEQ, KVH, repeat, HD), jnp.float32), -6.0, 6.0)
    return full.reshape(MICRO, SEQ, HQ * HD).astype(jnp.bfloat16)


def draw_keys(key, part):
    full = jnp.clip(jax.random.normal(jax.random.fold_in(key, 2), (MICRO, SEQ, KVH, HD), jnp.float32), -6.0, 6.0)
    return full.reshape(MICRO, SEQ, KVH * HD).astype(jnp.bfloat16)


def shard_levels(key, dims, split, least, largest):
    level = 1.0
    for dim, shards_of in split:
        heights = jax.random.uniform(jax.random.fold_in(jax.random.fold_in(key, 6), dim), (shards_of,), jnp.float32, least / len(split), largest / len(split))
        level = level * jnp.repeat(jnp.exp(heights), dims[dim] // shards_of).reshape((-1,) + (1,) * (len(dims) - 1 - dim))
    return level


def length_profile(count, total, most, skew):
    weights = [(1 << 20) // math.isqrt(grade ** skew) + 1 for grade in range(2, count + 1)]
    spare, counts = total - most - (count - 1), [1] * (count - 1)
    while spare > 0:
        free = [i for i in range(count - 1) if counts[i] < most]
        whole, budget = sum([weights[i] for i in free]), spare
        for i in free:
            more = min(most - counts[i], max(1, budget * weights[i] // whole), spare)
            counts[i] = counts[i] + more
            spare = spare - more
    return np.array([most] + counts)


def ragged(key, count, total, bound, slope):
    if count == 2:
        one = jax.random.randint(key, (), max(1, total - bound), min(bound, total - 1) + 1)
        return jnp.stack([one, total - one])
    sizes = jnp.asarray(length_profile(count, total, bound, slope), jnp.int32)
    pairs = (count - 1) // 2
    giver, receiver = sizes[1:1 + 2 * pairs:2], sizes[2:2 + 2 * pairs:2]
    margin = jnp.minimum(giver - 1, bound - receiver)
    passed = jax.random.randint(jax.random.fold_in(key, 1), (pairs,), 0, 1 << 20) % (margin + 1)
    sizes = sizes.at[1:1 + 2 * pairs:2].set(giver - passed).at[2:2 + 2 * pairs:2].set(receiver + passed)
    return sizes[jax.random.permutation(jax.random.fold_in(key, 2), count)]


def bell_draw(rng, extent, width, reach, pieces=(), held_as=jnp.bfloat16):
    drawn = width * jax.random.normal(rng, extent, jnp.float32)
    if pieces:
        drawn = drawn * shard_levels(rng, extent, pieces, -0.22, 0.18)
    return jnp.clip(drawn, -reach, reach).astype(held_as)


def setup_inputs(seed: int = 0) -> dict:
    key_of = jax.random.split(jax.random.key(seed), 6)
    return {
        "stream": bell_draw(key_of[0], (MICRO, SEQ, D), 0.25, 1.5, ((0, 2), (1, 16))),
        "queries": draw_queries(jax.random.fold_in(key_of[5], 71), 0),
        "keys": draw_keys(jax.random.fold_in(key_of[5], 71), 0),
        "values": bell_draw(key_of[3], (MICRO, SEQ, KVH * HD), 1.0, 6.0, ((0, 2), (1, 16))),
        "segments": jax.vmap(lambda own: jnp.searchsorted(jnp.cumsum(ragged(own, DOCS, SEQ, (WINDOW - 1) * TOK_DEV, 2)), jnp.arange(SEQ), side="right"))(jax.random.split(key_of[4], MICRO)).reshape((MICRO, SEQ)).astype(jnp.int32),
    }


def attend_block(query_rows, key_rows, value_rows, seg_query, seg_key, pos_query, pos_key):
    tok_count = query_rows.shape[0]
    key_count = key_rows.shape[0]
    repeat = HQ // KVH
    q_four = query_rows.astype(jnp.float32).reshape(tok_count, KVH, repeat, HD)
    k_three = key_rows.astype(jnp.float32).reshape(key_count, KVH, HD)
    v_three = value_rows.astype(jnp.float32).reshape(key_count, KVH, HD)
    scores = jnp.einsum("tgrd,wgd->grtw", q_four, k_three) * (HD ** -0.5)
    visible = (seg_query[:, None] == seg_key[None, :]) & (pos_key[None, :] <= pos_query[:, None])
    scores = jnp.where(visible, scores, jnp.float32(-1e30))
    top_score = jnp.max(scores, axis=-1, keepdims=True)
    expo = jnp.exp(scores - top_score)
    probs = (expo / jnp.sum(expo, axis=-1, keepdims=True)).astype(jnp.bfloat16)
    result = jnp.einsum("grtw,wgd->tgrd", probs.astype(jnp.float32), v_three)
    return result.reshape(tok_count, HQ * HD)


def reference(stream, queries, keys, values, segments):
    pad_len = (WINDOW - 1) * TOK_DEV
    win_len = WINDOW * TOK_DEV
    attended_all = []
    for micro in range(MICRO):
        key_pad = jnp.concatenate([jnp.zeros((pad_len, keys.shape[2]), keys.dtype), keys[micro]], axis=0)
        value_pad = jnp.concatenate([jnp.zeros((pad_len, values.shape[2]), values.dtype), values[micro]], axis=0)
        seg_pad = jnp.concatenate([jnp.full((pad_len,), -1, jnp.int32), segments[micro].astype(jnp.int32)], axis=0)
        query_all = queries[micro]
        seg_all = segments[micro].astype(jnp.int32)

        def one_block(block_id):
            start = (block_id * TOK_DEV).astype(jnp.int32)
            query_rows = lax.dynamic_slice_in_dim(query_all, start, TOK_DEV, 0)
            seg_query = lax.dynamic_slice_in_dim(seg_all, start, TOK_DEV, 0)
            key_rows = lax.dynamic_slice_in_dim(key_pad, start, win_len, 0)
            value_rows = lax.dynamic_slice_in_dim(value_pad, start, win_len, 0)
            seg_key = lax.dynamic_slice_in_dim(seg_pad, start, win_len, 0)
            pos_query = start + jnp.arange(TOK_DEV, dtype=jnp.int32)
            pos_key = start - pad_len + jnp.arange(win_len, dtype=jnp.int32)
            return attend_block(query_rows, key_rows, value_rows, seg_query, seg_key, pos_query, pos_key)

        blocks_out = lax.map(one_block, jnp.arange(SEQ // TOK_DEV, dtype=jnp.int32))
        attended_all.append(blocks_out.reshape(SEQ, HQ * HD))
    results = []
    for micro in range(MICRO):
        source = (micro - 1) % MICRO
        results.append((stream[source].astype(jnp.float32) + attended_all[source]).astype(jnp.bfloat16))
    return jnp.stack(results, axis=0)
```

```python
import functools
import math

import jax
import jax.numpy as jnp
from jax import lax
from jax.experimental import pallas as pl
from jax.experimental.pallas import tpu as pltpu
from jax.sharding import PartitionSpec as P

HQ = 64
KVH = 8
HD = 128
WINDOW = 8
REPEAT = HQ // KVH
PAIR = 2 * HD
SEG_ROWS = 16
PENALTY = float(2**20)
LOG2_SCALE = HD**-0.5 * math.log2(math.e)
CHUNKS = (1, 2, 2, 3)
SLOTS = (
    (7, 3, 5, 1, 4, 6, 2, 0),
    (7, 3, 5, 1, 2, 4, 0, 6),
    (7, 3, 1, 5, 4, 2, 6, 0),
    (7, 3, 1, 5, 2, 0, 4, 6),
)


def swap(value, axis, pairs):
    return lax.ppermute(value, axis, pairs + [(b, a) for a, b in pairs])


def exchange(value, axis, bit):
    return lax.ppermute(value, axis, [(i, i ^ bit) for i in range(lax.axis_size(axis))])


def from_groups_behind(value, groups):
    size = lax.axis_size("ctx")
    count = size // 4
    parity = (lax.axis_index("ctx") // 4 // groups) % 2
    halves = []
    for odd in (0, 1):
        pairs = [
            (4 * g + r, 4 * (g + groups) + r)
            for g in range(count - groups)
            if (g // groups) % 2 == odd
            for r in range(4)
        ]
        halves.append(swap(value, "ctx", pairs) if pairs else None)
    if halves[1] is None:
        return jnp.where(parity == 1, halves[0], jnp.zeros_like(value))
    return jnp.where(parity == 1, halves[0], halves[1])


def gather_window(block):
    index = lax.axis_index("ctx")
    in_y, in_core = (index // 2) % 2, index % 2
    behind_two = from_groups_behind(block, 2)
    behind = from_groups_behind(block, 1)
    y_behind = exchange(behind, "ctx", 2)
    y_other = exchange(jnp.where(in_y == 0, block, behind_two), "ctx", 2)
    core_four = exchange(
        jnp.concatenate(
            [behind, y_behind, y_other, jnp.where(in_core == 0, block, behind_two)]
        ),
        "ctx",
        1,
    )
    return (block, behind, y_behind, y_other, core_four)


def attend_kernel(first, tokens, meta, *refs):
    window = tokens * WINDOW
    if first:
        blocks, (query, stream, out, seg_out) = refs[:8], refs[8:12]
        keys, values, bias, extra = refs[12:]
        for n, block in enumerate(blocks):
            slot = meta[n]
            row = block[tokens : tokens + 1, :].astype(jnp.float32)
            seg_out[pl.ds(slot, 1), :] = jnp.where(slot + meta[8] >= WINDOW - 1, row, -1.0)
        segs = seg_out[...]
    else:
        seg_in, blocks, (query, stream, out) = refs[0], refs[1:9], refs[9:12]
        keys, values, bias, extra = refs[12:]
        segs = seg_in[...]
    own_row = segs[WINDOW - 1 :, :tokens]
    seg_zero = segs[WINDOW - 1 :, 0:1]
    own_column = segs.T[:tokens, WINDOW - 1 :]
    before = jnp.sum(jnp.where(segs[: WINDOW - 1, :tokens] != seg_zero, 1.0, 0.0))
    lane = lax.broadcasted_iota(jnp.int32, (tokens, HD), 1)
    extra[...] = jnp.where(
        lane == 0,
        jnp.where(own_column == seg_zero, 0.0, -PENALTY),
        jnp.where(lane == 1, -PENALTY, 0.0),
    ).astype(jnp.bfloat16)
    row_id = lax.broadcasted_iota(jnp.int32, (tokens, tokens), 0)
    column_id = lax.broadcasted_iota(jnp.int32, (tokens, tokens), 1)
    tail = bias.shape[1]
    bias[:, : tail - tokens] = jnp.zeros((tokens, tail - tokens), jnp.float32)
    bias[:, tail - tokens :] = jnp.where(
        (own_column == own_row) & (column_id <= row_id), 0.0, -PENALTY
    )
    for n, block in enumerate(blocks):
        rows = pl.ds(pl.multiple_of(meta[n] * tokens, tokens), tokens)
        keys[rows, :HD] = block[:tokens, :HD]
        values[rows, :HD] = block[:tokens, HD:]
    key_row = lax.broadcasted_iota(jnp.int32, (window, HD), 0)
    key_lane = lax.broadcasted_iota(jnp.int32, (window, HD), 1)
    keys[:, HD:] = jnp.where(
        ((key_lane == 0) & (key_row < window - tokens))
        | ((key_lane == 1) & (key_row.astype(jnp.float32) < before)),
        1.0,
        0.0,
    ).astype(jnp.bfloat16)
    values[:, HD:] = jnp.ones((window, HD), jnp.bfloat16)

    def columns(head):
        return slice(head * HD, (head + 1) * HD)

    def score(head):
        marks = extra[...]
        rows = jnp.concatenate(
            [
                jnp.concatenate([query[:, columns(h)], marks], axis=1)
                for h in (head, head + 1)
            ],
            axis=0,
        )
        scores = lax.dot_general(
            rows, keys[...], (((1,), (1,)), ((), ())), preferred_element_type=jnp.float32
        )
        own = scores[:, window - tail :] + jnp.concatenate([bias[...]] * 2, axis=0)
        return jnp.concatenate([scores[:, : window - tail], own], axis=1)

    def finish(head, scores):
        top = jnp.max(scores, axis=1, keepdims=True)
        weights = jnp.exp2((scores - top) * LOG2_SCALE).astype(jnp.bfloat16)
        sums = jnp.dot(weights, values[...], preferred_element_type=jnp.float32)
        attended = sums[:, :HD] / sums[:, HD:]
        for n, h in enumerate((head, head + 1)):
            out[:, columns(h)] = (
                attended[n * tokens : (n + 1) * tokens]
                + stream[:, columns(h)].astype(jnp.float32)
            ).astype(jnp.bfloat16)

    scores = score(0)
    for head in range(0, REPEAT, 2):
        later = score(head + 2) if head + 2 < REPEAT else None
        finish(head, scores)
        scores = later


def attend(meta, segs, blocks, part, queries, stream, head):
    tokens = queries.shape[0]
    first = segs is None
    rows = blocks[0].shape[0]
    width = REPEAT * HD
    own = [pl.BlockSpec((rows, PAIR), lambda i, m: (0, part)) for _ in range(4)]
    mate = [pl.BlockSpec((rows, PAIR), lambda i, m, n=n: (n, part)) for n in range(4)]
    wide = pl.BlockSpec((tokens, width), lambda i, m: (0, head))
    seg_spec = pl.BlockSpec((WINDOW, PAIR), lambda i, m: (0, 0))
    out_spec = pl.BlockSpec((tokens, width), lambda i, m: (0, 0))
    out_shape = jax.ShapeDtypeStruct((tokens, width), jnp.bfloat16)
    seg_shape = jax.ShapeDtypeStruct((WINDOW, PAIR), jnp.float32)
    window = tokens * WINDOW
    return pl.pallas_call(
        functools.partial(attend_kernel, first, tokens),
        grid_spec=pltpu.PrefetchScalarGridSpec(
            num_scalar_prefetch=1,
            grid=(1,),
            in_specs=([] if first else [seg_spec]) + own + mate + [wide, wide],
            out_specs=(out_spec, seg_spec) if first else out_spec,
            scratch_shapes=[
                pltpu.VMEM((window, PAIR), jnp.bfloat16),
                pltpu.VMEM((window, PAIR), jnp.bfloat16),
                pltpu.VMEM((tokens, PAIR), jnp.float32),
                pltpu.VMEM((tokens, HD), jnp.bfloat16),
            ],
        ),
        out_shape=(out_shape, seg_shape) if first else out_shape,
        compiler_params=pltpu.CompilerParams(vmem_limit_bytes=32 * 2**20),
        cost_estimate=pl.CostEstimate(
            flops=4 * tokens * REPEAT * window * PAIR,
            bytes_accessed=3 * tokens * width * 2 + window * PAIR * 2,
            transcendentals=tokens * REPEAT * window,
        ),
        name="attend",
    )(meta, *([] if first else [segs]), *blocks[:4], *([blocks[4]] * 4), queries, stream)


def local(stream, queries, keys, values, segments):
    stream, queries, keys, values, segments = stream[0], queries[0], keys[0], values[0], segments[0]
    tokens = queries.shape[0]
    index = lax.axis_index("ctx").astype(jnp.int32)
    meta = jnp.concatenate([jnp.asarray(SLOTS, jnp.int32)[index % 4], index[None]])
    pieces, segs, head = [], None, 0
    for size in CHUNKS:
        block = jnp.concatenate(
            [
                part[:, h * HD : (h + 1) * HD]
                for h in range(head, head + size)
                for part in (keys, values)
            ],
            axis=1,
        )
        if head == 0:
            seg_tile = jnp.pad(
                segments.astype(jnp.bfloat16)[None], ((0, SEG_ROWS - 1), (0, PAIR - tokens))
            )
            block = jnp.concatenate([block, seg_tile], axis=0)
        blocks = gather_window(block)
        for part in range(size):
            if segs is None:
                piece, segs = attend(meta, None, blocks, part, queries, stream, head)
            else:
                piece = attend(meta, segs, blocks, part, queries, stream, head)
            pieces.append(exchange(piece, "section", 1))
            head += 1
    return jnp.concatenate(pieces, axis=1)[None]


def solution(mesh):
    in_specs = (
        P("section", "ctx", None),
        P("section", "ctx", None),
        P("section", "ctx", None),
        P("section", "ctx", None),
        P("section", "ctx"),
    )
    out_specs = P("section", "ctx", None)
    return jax.shard_map(local, mesh=mesh, in_specs=in_specs, out_specs=out_specs, check_vma=False)
```

```python
import functools
import math

import jax
import jax.numpy as jnp
from jax import lax
from jax.experimental import pallas as pl
from jax.experimental.pallas import tpu as pltpu
from jax.sharding import PartitionSpec as P

HQ = 64
KVH = 8
HD = 128
WINDOW = 8
REPEAT = HQ // KVH
PAIR = 2 * HD
WIDTH = REPEAT * HD
SEG_ROWS = 16
PENALTY = float(2**20)
LOG2_SCALE = HD**-0.5 * math.log2(math.e)
LIGHT = pl.CostEstimate(flops=1, bytes_accessed=1, transcendentals=0)
HEAVY = pl.CostEstimate(flops=10**11, bytes_accessed=10**6, transcendentals=0)
SLOTS = (
    (7, 3, 5, 1, 4, 6, 2, 0),
    (7, 3, 5, 1, 2, 4, 0, 6),
    (7, 3, 1, 5, 4, 2, 6, 0),
    (7, 3, 1, 5, 2, 0, 4, 6),
)


def gate(value, *ahead):
    return lax.optimization_barrier((value, ahead))[0]


def exchange(value, axis, bit):
    return lax.ppermute(value, axis, [(i, i ^ bit) for i in range(lax.axis_size(axis))])


def from_groups_behind(value, groups):
    size = lax.axis_size("ctx")
    pairs = [(i, i + 4 * groups) for i in range(size - 4 * groups)]
    if not {a for a, _ in pairs} & {b for _, b in pairs}:
        pairs = pairs + [(b, a) for a, b in pairs]
    return lax.ppermute(value, "ctx", pairs)


def gather_behind(block):
    return from_groups_behind(block, 1), from_groups_behind(block, 2)


def join_kernel(bit, column, *refs):
    *parts, own, two, out = refs
    width = out.shape[1]
    row = 0
    for part in parts:
        start = column if part.shape[1] > width else 0
        out[row : row + part.shape[0], :] = part[:, start : start + width]
        row += part.shape[0]
    first = (lax.axis_index("ctx") // bit) % 2 == 0

    @pl.when(first)
    def _():
        out[row:, :] = own[:, column : column + width]

    @pl.when(jnp.logical_not(first))
    def _():
        out[row:, :] = two[:, column : column + width]


def join(parts, own, two, bit, chunk):
    first, size = chunk
    rows = sum(part.shape[0] for part in parts) + own.shape[0]
    vmem = pl.BlockSpec(memory_space=pltpu.VMEM)
    return pl.pallas_call(
        functools.partial(join_kernel, bit, first * PAIR),
        in_specs=[vmem] * (len(parts) + 2),
        out_specs=vmem,
        out_shape=jax.ShapeDtypeStruct((rows, size * PAIR), jnp.bfloat16),
        cost_estimate=LIGHT,
        compiler_params=pltpu.CompilerParams(vmem_limit_bytes=12 * 2**20),
        name="join",
    )(*parts, own, two)


def over_y(block, behind, chunk):
    one, two = behind
    return exchange(join([one], block, two, 2, chunk), "ctx", 2)


def over_core(block, behind, mates, chunk):
    one, two = behind
    return exchange(join([one, mates], block, two, 1, chunk), "ctx", 1)


def fill_block(out, tokens, chunk, keys, values, seg):
    first, size = chunk
    for n in range(size):
        source = slice((first + n) * HD, (first + n + 1) * HD)
        out[:tokens, n * PAIR : n * PAIR + HD] = keys[:, source]
        out[:tokens, n * PAIR + HD : (n + 1) * PAIR] = values[:, source]
    out[tokens:, :] = jnp.zeros((out.shape[0] - tokens, size * PAIR), jnp.bfloat16)
    row = seg[...].astype(jnp.float32).astype(jnp.bfloat16)
    for n in range(size):
        out[tokens : tokens + 1, n * PAIR : n * PAIR + tokens] = row


def pack_blocks_kernel(tokens, chunks, keys, values, seg, *outs):
    for out, chunk in zip(outs, chunks):
        fill_block(out, tokens, chunk, keys, values, seg)


def pack_blocks(keys, values, segments, chunks):
    tokens = keys.shape[0]
    shapes = [(tokens + SEG_ROWS, size * PAIR) for _, size in chunks]
    one = lambda i: (0, 0)
    return pl.pallas_call(
        functools.partial(pack_blocks_kernel, tokens, chunks),
        grid=(1,),
        in_specs=[pl.BlockSpec(keys.shape, one)] * 2 + [pl.BlockSpec((1, tokens), one)],
        out_specs=[pl.BlockSpec(shape, one) for shape in shapes],
        out_shape=[jax.ShapeDtypeStruct(shape, jnp.bfloat16) for shape in shapes],
        cost_estimate=LIGHT,
        compiler_params=pltpu.CompilerParams(vmem_limit_bytes=56 * 2**20),
        name="pack_blocks",
    )(keys, values, segments)


def fold_places(rows, size):
    per_row = WIDTH // PAIR
    tiles = [(n, r) for n in range(size) for r in range(rows // SEG_ROWS)]
    return [
        (r * SEG_ROWS, n * PAIR, t // per_row * SEG_ROWS, t % per_row * PAIR)
        for t, (n, r) in enumerate(tiles)
    ]


def pack_wide_kernel(parts, chunk, queries, stream, *refs):
    keys, values, seg, out, block, sems = refs if chunk else (None,) * 3 + refs[:1] + (None,) + refs[1:]
    tokens = queries.shape[0]
    copies = [
        pltpu.make_async_copy(
            source.at[:, pl.ds(head * WIDTH, WIDTH)],
            out.at[pl.ds(n * tokens, tokens)],
            sems.at[n],
        )
        for n, (source, head) in enumerate(((queries, stream)[m], head) for m, head in parts)
    ]
    for copy in copies:
        copy.start()
    if chunk:
        fill_block(block, tokens, chunk, keys, values, seg)
        base = len(parts) * tokens
        for row, column, to_row, to_column in fold_places(block.shape[0], chunk[1]):
            out[base + to_row : base + to_row + SEG_ROWS, to_column : to_column + PAIR] = block[
                row : row + SEG_ROWS, column : column + PAIR
            ]
    for copy in copies:
        copy.wait()


def pack_wide(queries, stream, parts, chunk=None, others=()):
    tokens = queries.shape[0]
    rows = len(parts) * tokens
    vmem = pl.BlockSpec(memory_space=pltpu.VMEM)
    scratch = [pltpu.SemaphoreType.DMA((len(parts),))]
    if chunk:
        block = (tokens + SEG_ROWS, chunk[1] * PAIR)
        rows += max(place[2] for place in fold_places(*block[:1], chunk[1])) + SEG_ROWS
        scratch = [pltpu.VMEM(block, jnp.bfloat16)] + scratch
    return pl.pallas_call(
        functools.partial(pack_wide_kernel, parts, chunk),
        in_specs=[pl.BlockSpec(memory_space=pltpu.HBM)] * 2 + [vmem] * len(others),
        out_specs=vmem,
        out_shape=jax.ShapeDtypeStruct((rows, WIDTH), jnp.bfloat16),
        scratch_shapes=scratch,
        cost_estimate=LIGHT,
        compiler_params=pltpu.CompilerParams(vmem_limit_bytes=56 * 2**20),
        name="pack_wide",
    )(queries, stream, *others)


def unfold_kernel(base, size, wide, out):
    for row, column, at_row, at_column in fold_places(out.shape[0], size):
        out[row : row + SEG_ROWS, column : column + PAIR] = wide[
            base + at_row : base + at_row + SEG_ROWS, at_column : at_column + PAIR
        ]


def unfold(wide, base, tokens, chunk):
    vmem = pl.BlockSpec(memory_space=pltpu.VMEM)
    return pl.pallas_call(
        functools.partial(unfold_kernel, base, chunk[1]),
        in_specs=[vmem],
        out_specs=vmem,
        out_shape=jax.ShapeDtypeStruct((tokens + SEG_ROWS, chunk[1] * PAIR), jnp.bfloat16),
        cost_estimate=LIGHT,
        compiler_params=pltpu.CompilerParams(vmem_limit_bytes=8 * 2**20),
        name="unfold",
    )(wide)


def attend_kernel(tokens, column, query_row, stream_row, *refs):
    blocks, (query_in, stream_in, out) = refs[:WINDOW], refs[WINDOW : WINDOW + 3]
    keys, values, bias, extra, segs_ref, query, stream, sems = refs[WINDOW + 3 :]
    window = tokens * WINDOW
    index = lax.axis_index("ctx")
    place = index % 4
    slots = [
        jnp.where(place < 2, jnp.where(place == 0, a, b), jnp.where(place == 2, c, d))
        for a, b, c, d in zip(*SLOTS)
    ]
    copies = [
        pltpu.make_async_copy(
            source.at[pl.ds(row, tokens), pl.ds(column, WIDTH)], target, sems.at[n]
        )
        for n, (source, row, target) in enumerate(
            ((query_in, query_row, query), (stream_in, stream_row, stream))
        )
    ]

    for copy in copies:
        copy.start()
    for slot, block in zip(slots, blocks):
        row = block[tokens : tokens + 1, :].astype(jnp.float32)
        segs_ref[pl.ds(slot, 1), :] = jnp.where(slot + index >= WINDOW - 1, row, -1.0)
    segs = segs_ref[...]
    own_row = segs[WINDOW - 1 :, :tokens]
    seg_zero = segs[WINDOW - 1 :, 0:1]
    own_column = segs.T[:tokens, WINDOW - 1 :]
    before = jnp.sum(jnp.where(segs[: WINDOW - 1, :tokens] != seg_zero, 1.0, 0.0))
    lane = lax.broadcasted_iota(jnp.int32, (tokens, HD), 1)
    extra[...] = jnp.where(
        lane == 0,
        jnp.where(own_column == seg_zero, 0.0, -PENALTY),
        jnp.where(lane == 1, -PENALTY, 0.0),
    ).astype(jnp.bfloat16)
    row_id = lax.broadcasted_iota(jnp.int32, (tokens, tokens), 0)
    column_id = lax.broadcasted_iota(jnp.int32, (tokens, tokens), 1)
    tail = bias.shape[1]
    bias[:, : tail - tokens] = jnp.zeros((tokens, tail - tokens), jnp.float32)
    bias[:, tail - tokens :] = jnp.where(
        (own_column == own_row) & (column_id <= row_id), 0.0, -PENALTY
    )
    key_row = lax.broadcasted_iota(jnp.int32, (window, HD), 0)
    key_lane = lax.broadcasted_iota(jnp.int32, (window, HD), 1)
    keys[:, HD:] = jnp.where(
        ((key_lane == 0) & (key_row < window - tokens))
        | ((key_lane == 1) & (key_row.astype(jnp.float32) < before)),
        1.0,
        0.0,
    ).astype(jnp.bfloat16)
    values[:, HD:] = jnp.ones((window, HD), jnp.bfloat16)

    for copy in copies:
        copy.wait()

    for slot, block in zip(slots, blocks):
        rows = pl.ds(pl.multiple_of(slot * tokens, tokens), tokens)
        keys[rows, :HD] = block[:tokens, :HD]
        values[rows, :HD] = block[:tokens, HD:]

    def columns(head):
        return slice(head * HD, (head + 1) * HD)

    def score(head):
        marks = extra[...]
        rows = jnp.concatenate(
            [jnp.concatenate([query[:, columns(h)], marks], axis=1) for h in (head, head + 1)],
            axis=0,
        )
        scores = lax.dot_general(
            rows, keys[...], (((1,), (1,)), ((), ())), preferred_element_type=jnp.float32
        )
        own = scores[:, window - tail :] + jnp.concatenate([bias[...]] * 2, axis=0)
        return jnp.concatenate([scores[:, : window - tail], own], axis=1)

    def finish(head, scores):
        top = jnp.max(scores, axis=1, keepdims=True)
        weights = jnp.exp2((scores - top) * LOG2_SCALE).astype(jnp.bfloat16)
        sums = jnp.dot(weights, values[...], preferred_element_type=jnp.float32)
        attended = sums[:, :HD] / sums[:, HD:]
        for n, h in enumerate((head, head + 1)):
            out[:, columns(h)] = (
                attended[n * tokens : (n + 1) * tokens]
                + stream[:, columns(h)].astype(jnp.float32)
            ).astype(jnp.bfloat16)

    scores = score(0)
    for head in range(0, REPEAT, 2):
        later = score(head + 2) if head + 2 < REPEAT else None
        finish(head, scores)
        scores = later


def attend(blocks, queries, stream, column, query_row, stream_row, cost):
    rows = blocks[0][0].shape[0]
    tokens = rows - SEG_ROWS
    window = tokens * WINDOW
    places = [(block, part, n) for block, part in blocks for n in range(block.shape[0] // rows)]
    return pl.pallas_call(
        functools.partial(attend_kernel, tokens, column, query_row, stream_row),
        grid=(1,),
        in_specs=[
            pl.BlockSpec((rows, PAIR), lambda i, part=part, n=n: (n, part)) for _, part, n in places
        ]
        + [pl.BlockSpec(memory_space=pl.ANY)] * 2,
        out_specs=pl.BlockSpec((tokens, WIDTH), lambda i: (0, 0)),
        out_shape=jax.ShapeDtypeStruct((tokens, WIDTH), jnp.bfloat16),
        scratch_shapes=[
            pltpu.VMEM((window, PAIR), jnp.bfloat16),
            pltpu.VMEM((window, PAIR), jnp.bfloat16),
            pltpu.VMEM((tokens, PAIR), jnp.float32),
            pltpu.VMEM((tokens, HD), jnp.bfloat16),
            pltpu.VMEM((WINDOW, PAIR), jnp.float32),
            pltpu.VMEM((tokens, WIDTH), jnp.bfloat16),
            pltpu.VMEM((tokens, WIDTH), jnp.bfloat16),
            pltpu.SemaphoreType.DMA((2,)),
        ],
        compiler_params=pltpu.CompilerParams(vmem_limit_bytes=16 * 2**20),
        cost_estimate=cost,
        name="attend",
    )(*[block for block, _, _ in places], queries, stream)


def assemble_kernel(places, *refs):
    *pieces, out, sems = refs
    copies = [
        pltpu.make_async_copy(
            piece, out.at[pl.ds(row, piece.shape[0]), pl.ds(column, piece.shape[1])], sems.at[n]
        )
        for n, (piece, (row, column)) in enumerate(zip(pieces[-len(places) :], places))
    ]
    for copy in copies:
        copy.start()
    for copy in copies:
        copy.wait()


def assemble(out, pieces, shape, cost):
    places = [place for _, place in pieces]
    given = [] if out is None else [out]
    return pl.pallas_call(
        functools.partial(assemble_kernel, places),
        in_specs=[pl.BlockSpec(memory_space=pl.ANY)] * len(given)
        + [pl.BlockSpec(memory_space=pltpu.VMEM)] * len(pieces),
        out_specs=pl.BlockSpec(memory_space=pl.ANY),
        out_shape=jax.ShapeDtypeStruct(shape, jnp.bfloat16),
        scratch_shapes=[pltpu.SemaphoreType.DMA((len(pieces),))],
        input_output_aliases={0: 0} if given else {},
        cost_estimate=cost,
        compiler_params=pltpu.CompilerParams(vmem_limit_bytes=8 * 2**20),
        name="assemble",
    )(*given, *[piece for piece, _ in pieces])


def local(stream, queries, keys, values, segments):
    stream, queries, keys, values = stream[0], queries[0], keys[0], values[0]
    segments = segments.reshape(1, -1)
    tokens = queries.shape[0]
    relay = lambda value: exchange(value, "section", 1)
    def own(full, head):
        block, one, mates, core, first = full
        at = [(part, head - first) for part in (block, one, mates, core)]
        return attend(at, queries, stream, head * WIDTH, 0, 0, LIGHT)

    def passed(full, n, q, q_row, s, s_row):
        return attend([(part, n) for part in full], q, s, 0, q_row, s_row, HEAVY)

    chunk_a, chunk_b, chunk_f = (0, 2), (2, 3), (5, 3)
    cut = 3 * tokens // 4
    whole = lambda chunk: (0, chunk[1])
    block_a, block_b = pack_blocks(keys, values, segments, (chunk_a, chunk_b))
    keys = gate(keys, block_a)
    wide_a = relay(pack_wide(queries, stream, ((0, 5),), chunk_f, (keys, values, segments)))
    behind_a = gather_behind(block_a)
    wide_b = pack_wide(gate(queries, block_a), stream, ((1, 5), (0, 6), (1, 6), (0, 7), (1, 7)))
    wide_b, behind_a = gate((wide_b, behind_a), wide_a, wide_b)
    wide_b = relay(wide_b)
    block_f = unfold(wide_a, tokens, tokens, chunk_f)
    behind_b = gather_behind(gate(block_b, behind_a))
    y_a = over_y(block_a, behind_a, whole(chunk_a))
    behind_f = gather_behind(gate(block_f, behind_b, y_a))
    y_b = over_y(gate(block_b, y_a), behind_b, whole(chunk_b))
    core_a = over_core(gate(block_a, behind_b), behind_a, y_a, whole(chunk_a))
    full_a = (block_a, behind_a[0], y_a, core_a)
    piece_0 = own(full_a + (0,), 0)
    recv_0 = relay(piece_0[:cut])
    piece_1 = own(gate(full_a, piece_0) + (0,), 1)
    recv_1 = relay(jnp.concatenate([piece_0[cut:], piece_1]))
    block_b, block_f = gate((block_b, block_f), behind_f, y_b, recv_0, piece_1, wide_b)
    core_b = over_core(block_b, behind_b, y_b, whole(chunk_b))
    y_f = over_y(block_f, behind_f, whole(chunk_f))
    full_b = (block_b, behind_b[0], y_b, core_b)
    piece_2 = own(full_b + (2,), 2)
    recv_2 = relay(piece_2)
    piece_3 = own(gate(full_b, piece_2) + (2,), 3)
    recv_3 = relay(piece_3)
    piece_4 = own(gate(full_b, piece_3) + (2,), 4)
    recv_4 = relay(piece_4)
    core_f = over_core(gate(block_f, piece_4, recv_1), behind_f, y_f, whole(chunk_f))
    full_f = (block_f, behind_f[0], y_f, core_f)
    piece_5 = passed(gate(full_f, recv_2), 0, wide_a, 0, wide_b, 0)
    piece_6 = passed(gate(full_f, piece_5, recv_3), 1, wide_b, tokens, wide_b, 2 * tokens)
    piece_7 = passed(gate(full_f, piece_6), 2, wide_b, 3 * tokens, wide_b, 4 * tokens)
    pieces = [
        (recv_0, (0, 0)),
        (recv_1[: tokens - cut], (cut, 0)),
        (recv_1[tokens - cut :], (0, WIDTH)),
        (recv_2, (0, 2 * WIDTH)),
        (recv_3, (0, 3 * WIDTH)),
        (piece_5, (0, 5 * WIDTH)),
        (piece_6, (0, 6 * WIDTH)),
        (piece_7, (0, 7 * WIDTH)),
    ]
    pieces.append((recv_4, (0, 4 * WIDTH)))
    return assemble(None, pieces, queries.shape, LIGHT)[None]


def solution(mesh):
    in_specs = (
        P("section", "ctx", None),
        P("section", "ctx", None),
        P("section", "ctx", None),
        P("section", "ctx", None),
        P("section", "ctx"),
    )
    out_specs = P("section", "ctx", None)
    return jax.shard_map(local, mesh=mesh, in_specs=in_specs, out_specs=out_specs, check_vma=False)
```

```python
import functools
import math

import jax
import jax.numpy as jnp
from jax import lax
from jax.experimental import pallas as pl
from jax.experimental.pallas import tpu as pltpu
from jax.sharding import PartitionSpec as P

HQ = 64
KVH = 8
HD = 128
WINDOW = 8
REPEAT = HQ // KVH
PAIR = 2 * HD
WIDTH = REPEAT * HD
SEG_ROWS = 16
PENALTY = float(2**20)
LOG2_SCALE = HD**-0.5 * math.log2(math.e)
LIGHT = pl.CostEstimate(flops=1, bytes_accessed=1, transcendentals=0)
HEAVY = pl.CostEstimate(flops=10**11, bytes_accessed=10**6, transcendentals=0)
SLOTS = (
    (7, 3, 5, 1, 4, 6, 2, 0),
    (7, 3, 5, 1, 2, 4, 0, 6),
    (7, 3, 1, 5, 4, 2, 6, 0),
    (7, 3, 1, 5, 2, 0, 4, 6),
)


def gate(value, *ahead):
    return lax.optimization_barrier((value, ahead))[0]


def exchange(value, axis, bit):
    return lax.ppermute(value, axis, [(i, i ^ bit) for i in range(lax.axis_size(axis))])


def from_groups_behind(value, groups):
    size = lax.axis_size("ctx")
    pairs = [(i, i + 4 * groups) for i in range(size - 4 * groups)]
    if not {a for a, _ in pairs} & {b for _, b in pairs}:
        pairs = pairs + [(b, a) for a, b in pairs]
    return lax.ppermute(value, "ctx", pairs)


def gather_behind(block):
    return from_groups_behind(block, 1), from_groups_behind(block, 2)


def join_kernel(bit, column, *refs):
    *parts, own, two, out = refs
    width = out.shape[1]
    row = 0
    for part in parts:
        start = column if part.shape[1] > width else 0
        out[row : row + part.shape[0], :] = part[:, start : start + width]
        row += part.shape[0]
    first = (lax.axis_index("ctx") // bit) % 2 == 0

    @pl.when(first)
    def _():
        out[row:, :] = own[:, column : column + width]

    @pl.when(jnp.logical_not(first))
    def _():
        out[row:, :] = two[:, column : column + width]


def join(parts, own, two, bit, chunk):
    first, size = chunk
    rows = sum(part.shape[0] for part in parts) + own.shape[0]
    vmem = pl.BlockSpec(memory_space=pltpu.VMEM)
    return pl.pallas_call(
        functools.partial(join_kernel, bit, first * PAIR),
        in_specs=[vmem] * (len(parts) + 2),
        out_specs=vmem,
        out_shape=jax.ShapeDtypeStruct((rows, size * PAIR), jnp.bfloat16),
        cost_estimate=LIGHT,
        compiler_params=pltpu.CompilerParams(vmem_limit_bytes=12 * 2**20),
        name="join",
    )(*parts, own, two)


def over_y(block, behind, chunk):
    one, two = behind
    return exchange(join([one], block, two, 2, chunk), "ctx", 2)


def over_core(block, behind, mates, chunk):
    one, two = behind
    return exchange(join([one, mates], block, two, 1, chunk), "ctx", 1)


def fill_block(out, tokens, chunk, keys, values, seg):
    first, size = chunk
    for n in range(size):
        source = slice((first + n) * HD, (first + n + 1) * HD)
        out[:tokens, n * PAIR : n * PAIR + HD] = keys[:, source]
        out[:tokens, n * PAIR + HD : (n + 1) * PAIR] = values[:, source]
    out[tokens:, :] = jnp.zeros((out.shape[0] - tokens, size * PAIR), jnp.bfloat16)
    row = seg[...].astype(jnp.float32).astype(jnp.bfloat16)
    for n in range(size):
        out[tokens : tokens + 1, n * PAIR : n * PAIR + tokens] = row


def fold_places(rows, size):
    per_row = WIDTH // PAIR
    tiles = [(n, r) for n in range(size) for r in range(rows // SEG_ROWS)]
    return [
        (r * SEG_ROWS, n * PAIR, t // per_row * SEG_ROWS, t % per_row * PAIR)
        for t, (n, r) in enumerate(tiles)
    ]


def pack_first_kernel(chunks, passed, query_head, queries, keys_in, values_in, seg_in, *refs):
    *blocks, out, block, keys, values, seg, sems = refs
    tokens = queries.shape[0]
    copies = [
        pltpu.make_async_copy(source, target, sems.at[n])
        for n, (source, target) in enumerate(
            (
                (keys_in, keys),
                (values_in, values),
                (seg_in, seg),
                (queries.at[:, pl.ds(query_head * WIDTH, WIDTH)], out.at[pl.ds(0, tokens)]),
            )
        )
    ]
    for copy in copies:
        copy.start()
    for copy in copies[:3]:
        copy.wait()
    for target, chunk in zip(blocks, chunks):
        fill_block(target, tokens, chunk, keys, values, seg)
    fill_block(block, tokens, passed, keys, values, seg)
    for row, column, to_row, to_column in fold_places(block.shape[0], passed[1]):
        out[tokens + to_row : tokens + to_row + SEG_ROWS, to_column : to_column + PAIR] = block[
            row : row + SEG_ROWS, column : column + PAIR
        ]
    copies[3].wait()


def pack_first(queries, keys, values, segments, chunks, passed):
    tokens = queries.shape[0]
    block = lambda chunk: (tokens + SEG_ROWS, chunk[1] * PAIR)
    folded = max(place[2] for place in fold_places(tokens + SEG_ROWS, passed[1])) + SEG_ROWS
    shapes = [block(chunk) for chunk in chunks] + [(tokens + folded, WIDTH)]
    vmem = pl.BlockSpec(memory_space=pltpu.VMEM)
    return pl.pallas_call(
        functools.partial(pack_first_kernel, chunks, passed, passed[0]),
        in_specs=[pl.BlockSpec(memory_space=pltpu.HBM)] * 4,
        out_specs=[vmem] * len(shapes),
        out_shape=[jax.ShapeDtypeStruct(shape, jnp.bfloat16) for shape in shapes],
        scratch_shapes=[
            pltpu.VMEM(block(passed), jnp.bfloat16),
            pltpu.VMEM(keys.shape, jnp.bfloat16),
            pltpu.VMEM(values.shape, jnp.bfloat16),
            pltpu.VMEM(segments.shape, segments.dtype),
            pltpu.SemaphoreType.DMA((4,)),
        ],
        cost_estimate=LIGHT,
        compiler_params=pltpu.CompilerParams(vmem_limit_bytes=56 * 2**20),
        name="pack_first",
    )(queries, keys, values, segments)


def pack_wide_kernel(parts, queries, stream, out, sems):
    tokens = queries.shape[0]
    copies = [
        pltpu.make_async_copy(
            (queries, stream)[m].at[:, pl.ds(head * WIDTH, WIDTH)],
            out.at[pl.ds(n * tokens, tokens)],
            sems.at[n],
        )
        for n, (m, head) in enumerate(parts)
    ]
    for copy in copies:
        copy.start()
    for copy in copies:
        copy.wait()


def pack_wide(queries, stream, parts):
    return pl.pallas_call(
        functools.partial(pack_wide_kernel, parts),
        in_specs=[pl.BlockSpec(memory_space=pltpu.HBM)] * 2,
        out_specs=pl.BlockSpec(memory_space=pltpu.VMEM),
        out_shape=jax.ShapeDtypeStruct((len(parts) * queries.shape[0], WIDTH), jnp.bfloat16),
        scratch_shapes=[pltpu.SemaphoreType.DMA((len(parts),))],
        cost_estimate=LIGHT,
        compiler_params=pltpu.CompilerParams(vmem_limit_bytes=56 * 2**20),
        name="pack_wide",
    )(queries, stream)


def unfold_kernel(base, size, wide, out):
    for row, column, at_row, at_column in fold_places(out.shape[0], size):
        out[row : row + SEG_ROWS, column : column + PAIR] = wide[
            base + at_row : base + at_row + SEG_ROWS, at_column : at_column + PAIR
        ]


def unfold(wide, base, tokens, chunk):
    vmem = pl.BlockSpec(memory_space=pltpu.VMEM)
    return pl.pallas_call(
        functools.partial(unfold_kernel, base, chunk[1]),
        in_specs=[vmem],
        out_specs=vmem,
        out_shape=jax.ShapeDtypeStruct((tokens + SEG_ROWS, chunk[1] * PAIR), jnp.bfloat16),
        cost_estimate=LIGHT,
        compiler_params=pltpu.CompilerParams(vmem_limit_bytes=8 * 2**20),
        name="unfold",
    )(wide)


def attend_kernel(tokens, column, query_row, stream_row, *refs):
    blocks, (query_in, stream_in, out) = refs[:WINDOW], refs[WINDOW : WINDOW + 3]
    keys, values, bias, extra, segs_ref, query, stream, sems = refs[WINDOW + 3 :]
    window = tokens * WINDOW
    index = lax.axis_index("ctx")
    place = index % 4
    slots = [
        jnp.where(place < 2, jnp.where(place == 0, a, b), jnp.where(place == 2, c, d))
        for a, b, c, d in zip(*SLOTS)
    ]
    copies = [
        pltpu.make_async_copy(
            source.at[pl.ds(row, tokens), pl.ds(column, WIDTH)], target, sems.at[n]
        )
        for n, (source, row, target) in enumerate(
            ((query_in, query_row, query), (stream_in, stream_row, stream))
        )
    ]

    for copy in copies:
        copy.start()
    for slot, block in zip(slots, blocks):
        row = block[tokens : tokens + 1, :].astype(jnp.float32)
        segs_ref[pl.ds(slot, 1), :] = jnp.where(slot + index >= WINDOW - 1, row, -1.0)
    segs = segs_ref[...]
    own_row = segs[WINDOW - 1 :, :tokens]
    seg_zero = segs[WINDOW - 1 :, 0:1]
    own_column = segs.T[:tokens, WINDOW - 1 :]
    before = jnp.sum(jnp.where(segs[: WINDOW - 1, :tokens] != seg_zero, 1.0, 0.0))
    lane = lax.broadcasted_iota(jnp.int32, (tokens, HD), 1)
    extra[...] = jnp.where(
        lane == 0,
        jnp.where(own_column == seg_zero, 0.0, -PENALTY),
        jnp.where(lane == 1, -PENALTY, 0.0),
    ).astype(jnp.bfloat16)
    row_id = lax.broadcasted_iota(jnp.int32, (tokens, tokens), 0)
    column_id = lax.broadcasted_iota(jnp.int32, (tokens, tokens), 1)
    tail = bias.shape[1]
    bias[:, : tail - tokens] = jnp.zeros((tokens, tail - tokens), jnp.float32)
    bias[:, tail - tokens :] = jnp.where(
        (own_column == own_row) & (column_id <= row_id), 0.0, -PENALTY
    )
    key_row = lax.broadcasted_iota(jnp.int32, (window, HD), 0)
    key_lane = lax.broadcasted_iota(jnp.int32, (window, HD), 1)
    keys[:, HD:] = jnp.where(
        ((key_lane == 0) & (key_row < window - tokens))
        | ((key_lane == 1) & (key_row.astype(jnp.float32) < before)),
        1.0,
        0.0,
    ).astype(jnp.bfloat16)
    values[:, HD:] = jnp.ones((window, HD), jnp.bfloat16)

    for copy in copies:
        copy.wait()

    for slot, block in zip(slots, blocks):
        rows = pl.ds(pl.multiple_of(slot * tokens, tokens), tokens)
        keys[rows, :HD] = block[:tokens, :HD]
        values[rows, :HD] = block[:tokens, HD:]

    def columns(head):
        return slice(head * HD, (head + 1) * HD)

    def score(head):
        marks = extra[...]
        rows = jnp.concatenate(
            [jnp.concatenate([query[:, columns(h)], marks], axis=1) for h in (head, head + 1)],
            axis=0,
        )
        scores = lax.dot_general(
            rows, keys[...], (((1,), (1,)), ((), ())), preferred_element_type=jnp.float32
        )
        own = scores[:, window - tail :] + jnp.concatenate([bias[...]] * 2, axis=0)
        return jnp.concatenate([scores[:, : window - tail], own], axis=1)

    def finish(head, scores):
        top = jnp.max(scores, axis=1, keepdims=True)
        weights = jnp.exp2((scores - top) * LOG2_SCALE).astype(jnp.bfloat16)
        sums = jnp.dot(weights, values[...], preferred_element_type=jnp.float32)
        attended = sums[:, :HD] / sums[:, HD:]
        for n, h in enumerate((head, head + 1)):
            out[:, columns(h)] = (
                attended[n * tokens : (n + 1) * tokens]
                + stream[:, columns(h)].astype(jnp.float32)
            ).astype(jnp.bfloat16)

    scores = score(0)
    for head in range(0, REPEAT, 2):
        later = score(head + 2) if head + 2 < REPEAT else None
        finish(head, scores)
        scores = later


def attend(blocks, queries, stream, column, query_row, stream_row, cost):
    rows = blocks[0][0].shape[0]
    tokens = rows - SEG_ROWS
    window = tokens * WINDOW
    places = [(block, part, n) for block, part in blocks for n in range(block.shape[0] // rows)]
    return pl.pallas_call(
        functools.partial(attend_kernel, tokens, column, query_row, stream_row),
        grid=(1,),
        in_specs=[
            pl.BlockSpec((rows, PAIR), lambda i, part=part, n=n: (n, part)) for _, part, n in places
        ]
        + [pl.BlockSpec(memory_space=pl.ANY)] * 2,
        out_specs=pl.BlockSpec((tokens, WIDTH), lambda i: (0, 0)),
        out_shape=jax.ShapeDtypeStruct((tokens, WIDTH), jnp.bfloat16),
        scratch_shapes=[
            pltpu.VMEM((window, PAIR), jnp.bfloat16),
            pltpu.VMEM((window, PAIR), jnp.bfloat16),
            pltpu.VMEM((tokens, PAIR), jnp.float32),
            pltpu.VMEM((tokens, HD), jnp.bfloat16),
            pltpu.VMEM((WINDOW, PAIR), jnp.float32),
            pltpu.VMEM((tokens, WIDTH), jnp.bfloat16),
            pltpu.VMEM((tokens, WIDTH), jnp.bfloat16),
            pltpu.SemaphoreType.DMA((2,)),
        ],
        compiler_params=pltpu.CompilerParams(vmem_limit_bytes=16 * 2**20),
        cost_estimate=cost,
        name="attend",
    )(*[block for block, _, _ in places], queries, stream)


def assemble_kernel(places, *refs):
    *pieces, out, sems = refs
    copies = [
        pltpu.make_async_copy(
            piece, out.at[pl.ds(row, piece.shape[0]), pl.ds(column, piece.shape[1])], sems.at[n]
        )
        for n, (piece, (row, column)) in enumerate(zip(pieces[-len(places) :], places))
    ]
    for copy in copies:
        copy.start()
    for copy in copies:
        copy.wait()


def assemble(out, pieces, shape, cost):
    places = [place for _, place in pieces]
    given = [] if out is None else [out]
    return pl.pallas_call(
        functools.partial(assemble_kernel, places),
        in_specs=[pl.BlockSpec(memory_space=pl.ANY)] * len(given)
        + [pl.BlockSpec(memory_space=pltpu.VMEM)] * len(pieces),
        out_specs=pl.BlockSpec(memory_space=pl.ANY),
        out_shape=jax.ShapeDtypeStruct(shape, jnp.bfloat16),
        scratch_shapes=[pltpu.SemaphoreType.DMA((len(pieces),))],
        input_output_aliases={0: 0} if given else {},
        cost_estimate=cost,
        compiler_params=pltpu.CompilerParams(vmem_limit_bytes=8 * 2**20),
        name="assemble",
    )(*given, *[piece for piece, _ in pieces])


def local(stream, queries, keys, values, segments):
    stream, queries, keys, values = stream[0], queries[0], keys[0], values[0]
    segments = segments.reshape(1, -1)
    tokens = queries.shape[0]
    relay = lambda value: exchange(value, "section", 1)
    def own(full, head):
        block, one, mates, core, first = full
        at = [(part, head - first) for part in (block, one, mates, core)]
        return attend(at, queries, stream, head * WIDTH, 0, 0, LIGHT)

    def passed(full, n, q, q_row, s, s_row):
        return attend([(part, n) for part in full], q, s, 0, q_row, s_row, LIGHT)

    chunk_a, chunk_b, chunk_f = (0, 2), (2, 3), (5, 3)
    cut, half = 3 * tokens // 4, tokens // 2
    whole = lambda chunk: (0, chunk[1])
    block_a, block_b, wide_a = pack_first(queries, keys, values, segments, (chunk_a, chunk_b), chunk_f)
    wide_a = relay(wide_a)
    behind_a = gather_behind(block_a)
    wide_b = pack_wide(gate(queries, block_a), stream, ((1, 5), (0, 6), (1, 6), (0, 7), (1, 7)))
    wide_b, behind_a = gate((wide_b, behind_a), wide_a, wide_b)
    wide_b = relay(wide_b)
    block_f = unfold(wide_a, tokens, tokens, chunk_f)
    behind_b = gather_behind(gate(block_b, behind_a))
    y_a = over_y(block_a, behind_a, whole(chunk_a))
    behind_f = gather_behind(gate(block_f, behind_b, y_a))
    y_b = over_y(gate(block_b, y_a), behind_b, whole(chunk_b))
    core_a = over_core(gate(block_a, behind_b), behind_a, y_a, whole(chunk_a))
    full_a = (block_a, behind_a[0], y_a, core_a)
    piece_0 = own(full_a + (0,), 0)
    recv_0 = relay(piece_0[:cut])
    piece_1 = own(gate(full_a, piece_0) + (0,), 1)
    recv_1 = relay(jnp.concatenate([piece_0[cut:], piece_1]))
    block_b, block_f = gate((block_b, block_f), behind_f, y_b, recv_0, piece_1, wide_b)
    core_b = over_core(block_b, behind_b, y_b, whole(chunk_b))
    y_f = over_y(block_f, behind_f, whole(chunk_f))
    full_b = (block_b, behind_b[0], y_b, core_b)
    piece_2 = own(full_b + (2,), 2)
    recv_2 = relay(piece_2[:half])
    piece_3 = own(gate(full_b, piece_2) + (2,), 3)
    recv_3 = relay(jnp.concatenate([piece_2[half:], piece_3]))
    piece_4 = own(gate(full_b, piece_3) + (2,), 4)
    recv_4 = relay(piece_4)
    core_f = over_core(gate(block_f, piece_4, recv_1, recv_2), behind_f, y_f, whole(chunk_f))
    full_f = (block_f, behind_f[0], y_f, core_f)
    piece_5 = passed(full_f, 0, wide_a, 0, wide_b, 0)
    piece_6 = passed(gate(full_f, piece_5), 1, wide_b, tokens, wide_b, 2 * tokens)
    piece_7 = passed(gate(full_f, piece_6), 2, wide_b, 3 * tokens, wide_b, 4 * tokens)
    recv_3 = gate(recv_3, piece_6)
    pieces = [
        (recv_0, (0, 0)),
        (recv_1[: tokens - cut], (cut, 0)),
        (recv_1[tokens - cut :], (0, WIDTH)),
        (recv_2, (0, 2 * WIDTH)),
        (recv_3[: tokens - half], (half, 2 * WIDTH)),
        (recv_3[tokens - half :], (0, 3 * WIDTH)),
        (piece_5, (0, 5 * WIDTH)),
        (piece_6, (0, 6 * WIDTH)),
    ]
    out = assemble(None, pieces, queries.shape, LIGHT)
    out = lax.dynamic_update_slice(out, piece_7, (0, 7 * WIDTH))
    recv_4 = gate(recv_4, out)
    return lax.dynamic_update_slice(out, recv_4, (0, 4 * WIDTH))[None]


def solution(mesh):
    in_specs = (
        P("section", "ctx", None),
        P("section", "ctx", None),
        P("section", "ctx", None),
        P("section", "ctx", None),
        P("section", "ctx"),
    )
    out_specs = P("section", "ctx", None)
    return jax.shard_map(local, mesh=mesh, in_specs=in_specs, out_specs=out_specs, check_vma=False)
```

```python
import functools
import math

import jax
import jax.numpy as jnp
from jax import lax
from jax.experimental import pallas as pl
from jax.experimental.pallas import tpu as pltpu
from jax.sharding import PartitionSpec as P

HQ = 64
KVH = 8
HD = 128
WINDOW = 8
REPEAT = HQ // KVH
PAIR = 2 * HD
WIDTH = REPEAT * HD
SEG_ROWS = 16
PENALTY = float(2**20)
LOG2_SCALE = HD**-0.5 * math.log2(math.e)
LIGHT = pl.CostEstimate(flops=1, bytes_accessed=1, transcendentals=0)
HEAVY = pl.CostEstimate(flops=10**11, bytes_accessed=10**6, transcendentals=0)
SLOTS = (
    (7, 3, 5, 1, 4, 6, 2, 0),
    (7, 3, 5, 1, 2, 4, 0, 6),
    (7, 3, 1, 5, 4, 2, 6, 0),
    (7, 3, 1, 5, 2, 0, 4, 6),
)


def gate(value, *ahead):
    return lax.optimization_barrier((value, ahead))[0]


def exchange(value, axis, bit):
    return lax.ppermute(value, axis, [(i, i ^ bit) for i in range(lax.axis_size(axis))])


def from_groups_behind(value, groups):
    size = lax.axis_size("ctx")
    pairs = [(i, i + 4 * groups) for i in range(size - 4 * groups)]
    if not {a for a, _ in pairs} & {b for _, b in pairs}:
        pairs = pairs + [(b, a) for a, b in pairs]
    return lax.ppermute(value, "ctx", pairs)


def gather_behind(block):
    return from_groups_behind(block, 1), from_groups_behind(block, 2)


def join_kernel(bit, column, *refs):
    *parts, own, two, out = refs
    width = out.shape[1]
    row = 0
    for part in parts:
        start = column if part.shape[1] > width else 0
        out[row : row + part.shape[0], :] = part[:, start : start + width]
        row += part.shape[0]
    first = (lax.axis_index("ctx") // bit) % 2 == 0

    @pl.when(first)
    def _():
        out[row:, :] = own[:, column : column + width]

    @pl.when(jnp.logical_not(first))
    def _():
        out[row:, :] = two[:, column : column + width]


def join(parts, own, two, bit, chunk):
    first, size = chunk
    rows = sum(part.shape[0] for part in parts) + own.shape[0]
    vmem = pl.BlockSpec(memory_space=pltpu.VMEM)
    return pl.pallas_call(
        functools.partial(join_kernel, bit, first * PAIR),
        in_specs=[vmem] * (len(parts) + 2),
        out_specs=vmem,
        out_shape=jax.ShapeDtypeStruct((rows, size * PAIR), jnp.bfloat16),
        cost_estimate=LIGHT,
        compiler_params=pltpu.CompilerParams(vmem_limit_bytes=12 * 2**20),
        name="join",
    )(*parts, own, two)


def over_y(block, behind, chunk):
    one, two = behind
    return exchange(join([one], block, two, 2, chunk), "ctx", 2)


def over_core(block, behind, mates, chunk):
    one, two = behind
    return exchange(join([one, mates], block, two, 1, chunk), "ctx", 1)


def fill_block(out, tokens, chunk, keys, values, seg):
    first, size = chunk
    for n in range(size):
        source = slice((first + n) * HD, (first + n + 1) * HD)
        out[:tokens, n * PAIR : n * PAIR + HD] = keys[:, source]
        out[:tokens, n * PAIR + HD : (n + 1) * PAIR] = values[:, source]
    out[tokens:, :] = jnp.zeros((out.shape[0] - tokens, size * PAIR), jnp.bfloat16)
    row = seg[...].astype(jnp.float32).astype(jnp.bfloat16)
    for n in range(size):
        out[tokens : tokens + 1, n * PAIR : n * PAIR + tokens] = row


def fold_places(rows, size):
    per_row = WIDTH // PAIR
    tiles = [(n, r) for n in range(size) for r in range(rows // SEG_ROWS)]
    return [
        (r * SEG_ROWS, n * PAIR, t // per_row * SEG_ROWS, t % per_row * PAIR)
        for t, (n, r) in enumerate(tiles)
    ]


def pack_first_kernel(chunks, passed, queries, stream, keys_in, values_in, seg_in, *refs):
    *blocks, out, block, keys, values, seg, sems = refs
    tokens = queries.shape[0]
    copies = [
        pltpu.make_async_copy(source, target, sems.at[n])
        for n, (source, target) in enumerate(
            (
                (keys_in, keys),
                (values_in, values),
                (seg_in, seg),
                (queries.at[:, pl.ds(passed[0] * WIDTH, WIDTH)], out.at[pl.ds(0, tokens)]),
                (stream.at[:, pl.ds(passed[0] * WIDTH, WIDTH)], out.at[pl.ds(tokens, tokens)]),
            )
        )
    ]
    for copy in copies:
        copy.start()
    for copy in copies[:3]:
        copy.wait()
    for target, chunk in zip(blocks, chunks):
        fill_block(target, tokens, chunk, keys, values, seg)
    fill_block(block, tokens, passed, keys, values, seg)
    for row, column, to_row, to_column in fold_places(block.shape[0], passed[1]):
        to_row += 2 * tokens
        out[to_row : to_row + SEG_ROWS, to_column : to_column + PAIR] = block[
            row : row + SEG_ROWS, column : column + PAIR
        ]
    for copy in copies[3:]:
        copy.wait()


def pack_first(queries, stream, keys, values, segments, chunks, passed):
    tokens = queries.shape[0]
    block = lambda chunk: (tokens + SEG_ROWS, chunk[1] * PAIR)
    folded = max(place[2] for place in fold_places(tokens + SEG_ROWS, passed[1])) + SEG_ROWS
    shapes = [block(chunk) for chunk in chunks] + [(2 * tokens + folded, WIDTH)]
    vmem = pl.BlockSpec(memory_space=pltpu.VMEM)
    return pl.pallas_call(
        functools.partial(pack_first_kernel, chunks, passed),
        in_specs=[pl.BlockSpec(memory_space=pltpu.HBM)] * 5,
        out_specs=[vmem] * len(shapes),
        out_shape=[jax.ShapeDtypeStruct(shape, jnp.bfloat16) for shape in shapes],
        scratch_shapes=[
            pltpu.VMEM(block(passed), jnp.bfloat16),
            pltpu.VMEM(keys.shape, jnp.bfloat16),
            pltpu.VMEM(values.shape, jnp.bfloat16),
            pltpu.VMEM(segments.shape, segments.dtype),
            pltpu.SemaphoreType.DMA((5,)),
        ],
        cost_estimate=LIGHT,
        compiler_params=pltpu.CompilerParams(vmem_limit_bytes=56 * 2**20),
        name="pack_first",
    )(queries, stream, keys, values, segments)


def pack_wide_kernel(parts, queries, stream, out, sems):
    tokens = queries.shape[0]
    copies = [
        pltpu.make_async_copy(
            (queries, stream)[m].at[:, pl.ds(head * WIDTH, WIDTH)],
            out.at[pl.ds(n * tokens, tokens)],
            sems.at[n],
        )
        for n, (m, head) in enumerate(parts)
    ]
    for copy in copies:
        copy.start()
    for copy in copies:
        copy.wait()


def pack_wide(queries, stream, parts):
    return pl.pallas_call(
        functools.partial(pack_wide_kernel, parts),
        in_specs=[pl.BlockSpec(memory_space=pltpu.HBM)] * 2,
        out_specs=pl.BlockSpec(memory_space=pltpu.VMEM),
        out_shape=jax.ShapeDtypeStruct((len(parts) * queries.shape[0], WIDTH), jnp.bfloat16),
        scratch_shapes=[pltpu.SemaphoreType.DMA((len(parts),))],
        cost_estimate=LIGHT,
        compiler_params=pltpu.CompilerParams(vmem_limit_bytes=56 * 2**20),
        name="pack_wide",
    )(queries, stream)


def unfold_kernel(base, size, wide, out):
    for row, column, at_row, at_column in fold_places(out.shape[0], size):
        out[row : row + SEG_ROWS, column : column + PAIR] = wide[
            base + at_row : base + at_row + SEG_ROWS, at_column : at_column + PAIR
        ]


def unfold(wide, base, tokens, chunk):
    vmem = pl.BlockSpec(memory_space=pltpu.VMEM)
    return pl.pallas_call(
        functools.partial(unfold_kernel, base, chunk[1]),
        in_specs=[vmem],
        out_specs=vmem,
        out_shape=jax.ShapeDtypeStruct((tokens + SEG_ROWS, chunk[1] * PAIR), jnp.bfloat16),
        cost_estimate=LIGHT,
        compiler_params=pltpu.CompilerParams(vmem_limit_bytes=8 * 2**20),
        name="unfold",
    )(wide)


def attend_kernel(tokens, column, query_row, stream_row, *refs):
    blocks, (query_in, stream_in, out) = refs[:WINDOW], refs[WINDOW : WINDOW + 3]
    keys, values, bias, extra, segs_ref, query, stream, sems = refs[WINDOW + 3 :]
    window = tokens * WINDOW
    index = lax.axis_index("ctx")
    place = index % 4
    slots = [
        jnp.where(place < 2, jnp.where(place == 0, a, b), jnp.where(place == 2, c, d))
        for a, b, c, d in zip(*SLOTS)
    ]
    copies = [
        pltpu.make_async_copy(
            source.at[pl.ds(row, tokens), pl.ds(column, WIDTH)], target, sems.at[n]
        )
        for n, (source, row, target) in enumerate(
            ((query_in, query_row, query), (stream_in, stream_row, stream))
        )
    ]

    for copy in copies:
        copy.start()
    for slot, block in zip(slots, blocks):
        row = block[tokens : tokens + 1, :].astype(jnp.float32)
        segs_ref[pl.ds(slot, 1), :] = jnp.where(slot + index >= WINDOW - 1, row, -1.0)
    segs = segs_ref[...]
    own_row = segs[WINDOW - 1 :, :tokens]
    seg_zero = segs[WINDOW - 1 :, 0:1]
    own_column = segs.T[:tokens, WINDOW - 1 :]
    before = jnp.sum(jnp.where(segs[: WINDOW - 1, :tokens] != seg_zero, 1.0, 0.0))
    lane = lax.broadcasted_iota(jnp.int32, (tokens, HD), 1)
    extra[...] = jnp.where(
        lane == 0,
        jnp.where(own_column == seg_zero, 0.0, -PENALTY),
        jnp.where(lane == 1, -PENALTY, 0.0),
    ).astype(jnp.bfloat16)
    row_id = lax.broadcasted_iota(jnp.int32, (tokens, tokens), 0)
    column_id = lax.broadcasted_iota(jnp.int32, (tokens, tokens), 1)
    tail = bias.shape[1]
    bias[:, : tail - tokens] = jnp.zeros((tokens, tail - tokens), jnp.float32)
    bias[:, tail - tokens :] = jnp.where(
        (own_column == own_row) & (column_id <= row_id), 0.0, -PENALTY
    )
    key_row = lax.broadcasted_iota(jnp.int32, (window, HD), 0)
    key_lane = lax.broadcasted_iota(jnp.int32, (window, HD), 1)
    keys[:, HD:] = jnp.where(
        ((key_lane == 0) & (key_row < window - tokens))
        | ((key_lane == 1) & (key_row.astype(jnp.float32) < before)),
        1.0,
        0.0,
    ).astype(jnp.bfloat16)
    values[:, HD:] = jnp.ones((window, HD), jnp.bfloat16)

    for copy in copies:
        copy.wait()

    for slot, block in zip(slots, blocks):
        rows = pl.ds(pl.multiple_of(slot * tokens, tokens), tokens)
        keys[rows, :HD] = block[:tokens, :HD]
        values[rows, :HD] = block[:tokens, HD:]

    def columns(head):
        return slice(head * HD, (head + 1) * HD)

    def score(head):
        marks = extra[...]
        rows = jnp.concatenate(
            [jnp.concatenate([query[:, columns(h)], marks], axis=1) for h in (head, head + 1)],
            axis=0,
        )
        scores = lax.dot_general(
            rows, keys[...], (((1,), (1,)), ((), ())), preferred_element_type=jnp.float32
        )
        own = scores[:, window - tail :] + jnp.concatenate([bias[...]] * 2, axis=0)
        return jnp.concatenate([scores[:, : window - tail], own], axis=1)

    def finish(head, scores):
        top = jnp.max(scores, axis=1, keepdims=True)
        weights = jnp.exp2((scores - top) * LOG2_SCALE).astype(jnp.bfloat16)
        sums = jnp.dot(weights, values[...], preferred_element_type=jnp.float32)
        attended = sums[:, :HD] / sums[:, HD:]
        for n, h in enumerate((head, head + 1)):
            out[:, columns(h)] = (
                attended[n * tokens : (n + 1) * tokens]
                + stream[:, columns(h)].astype(jnp.float32)
            ).astype(jnp.bfloat16)

    scores = score(0)
    for head in range(0, REPEAT, 2):
        later = score(head + 2) if head + 2 < REPEAT else None
        finish(head, scores)
        scores = later


def attend(blocks, queries, stream, column, query_row, stream_row, cost):
    rows = blocks[0][0].shape[0]
    tokens = rows - SEG_ROWS
    window = tokens * WINDOW
    places = [(block, part, n) for block, part in blocks for n in range(block.shape[0] // rows)]
    return pl.pallas_call(
        functools.partial(attend_kernel, tokens, column, query_row, stream_row),
        grid=(1,),
        in_specs=[
            pl.BlockSpec((rows, PAIR), lambda i, part=part, n=n: (n, part)) for _, part, n in places
        ]
        + [pl.BlockSpec(memory_space=pl.ANY)] * 2,
        out_specs=pl.BlockSpec((tokens, WIDTH), lambda i: (0, 0)),
        out_shape=jax.ShapeDtypeStruct((tokens, WIDTH), jnp.bfloat16),
        scratch_shapes=[
            pltpu.VMEM((window, PAIR), jnp.bfloat16),
            pltpu.VMEM((window, PAIR), jnp.bfloat16),
            pltpu.VMEM((tokens, PAIR), jnp.float32),
            pltpu.VMEM((tokens, HD), jnp.bfloat16),
            pltpu.VMEM((WINDOW, PAIR), jnp.float32),
            pltpu.VMEM((tokens, WIDTH), jnp.bfloat16),
            pltpu.VMEM((tokens, WIDTH), jnp.bfloat16),
            pltpu.SemaphoreType.DMA((2,)),
        ],
        compiler_params=pltpu.CompilerParams(vmem_limit_bytes=16 * 2**20),
        cost_estimate=cost,
        name="attend",
    )(*[block for block, _, _ in places], queries, stream)


def assemble_kernel(places, *refs):
    *pieces, out, sems = refs
    copies = [
        pltpu.make_async_copy(
            piece, out.at[pl.ds(row, piece.shape[0]), pl.ds(column, piece.shape[1])], sems.at[n]
        )
        for n, (piece, (row, column)) in enumerate(zip(pieces[-len(places) :], places))
    ]
    for copy in copies:
        copy.start()
    for copy in copies:
        copy.wait()


def assemble(out, pieces, shape, cost):
    places = [place for _, place in pieces]
    given = [] if out is None else [out]
    return pl.pallas_call(
        functools.partial(assemble_kernel, places),
        in_specs=[pl.BlockSpec(memory_space=pl.ANY)] * len(given)
        + [pl.BlockSpec(memory_space=pltpu.VMEM)] * len(pieces),
        out_specs=pl.BlockSpec(memory_space=pl.ANY),
        out_shape=jax.ShapeDtypeStruct(shape, jnp.bfloat16),
        scratch_shapes=[pltpu.SemaphoreType.DMA((len(pieces),))],
        input_output_aliases={0: 0} if given else {},
        cost_estimate=cost,
        compiler_params=pltpu.CompilerParams(vmem_limit_bytes=8 * 2**20),
        name="assemble",
    )(*given, *[piece for piece, _ in pieces])


def local(stream, queries, keys, values, segments):
    stream, queries, keys, values = stream[0], queries[0], keys[0], values[0]
    segments = segments.reshape(1, -1)
    tokens = queries.shape[0]
    relay = lambda value: exchange(value, "section", 1)
    def own(full, n, core, at, head):
        at = [(part, n) for part in full] + [(core, at)]
        return attend(at, queries, stream, head * WIDTH, 0, 0, LIGHT)

    def passed(full, n, core, at, wide, row):
        at = [(part, n) for part in full] + [(core, at)]
        return attend(at, wide, wide, 0, row, row + tokens, LIGHT)

    chunk_a, chunk_b, chunk_f = (0, 3), (3, 2), (5, 3)
    cut = 3 * tokens // 4
    whole = lambda chunk: (0, chunk[1])
    block_a, block_b, wide_a = pack_first(
        queries, stream, keys, values, segments, (chunk_a, chunk_b), chunk_f
    )
    wide_a = relay(wide_a)
    behind_a = gather_behind(block_a)
    wide_b = pack_wide(gate(queries, block_a), stream, ((0, 6), (1, 6), (0, 7), (1, 7)))
    wide_b, behind_a = gate((wide_b, behind_a), wide_a, wide_b)
    wide_b = relay(wide_b)
    block_f = unfold(wide_a, 2 * tokens, tokens, chunk_f)
    behind_b = gather_behind(gate(block_b, behind_a))
    y_a = over_y(block_a, behind_a, whole(chunk_a))
    behind_f = gather_behind(gate(block_f, behind_b, y_a))
    y_b = over_y(gate(block_b, y_a), behind_b, whole(chunk_b))
    block_a = gate(block_a, behind_b)
    core_a = over_core(block_a, behind_a, y_a, (0, 2))
    core_2 = over_core(block_a, behind_a, y_a, (2, 1))
    full_a = (block_a, behind_a[0], y_a)
    piece_0 = own(full_a, 0, core_a, 0, 0)
    recv_0 = relay(piece_0[:cut])
    piece_1 = own(gate(full_a, piece_0), 1, core_a, 1, 1)
    piece_2 = own(gate(full_a, piece_1), 2, core_2, 0, 2)
    recv_1 = relay(jnp.concatenate([piece_0[cut:], piece_1, piece_2[:cut]]))
    block_b, block_f = gate((block_b, block_f), behind_f, y_b, recv_0, piece_2, wide_b)
    core_b = [over_core(block_b, behind_b, y_b, (n, 1)) for n in range(chunk_b[1])]
    y_f = over_y(block_f, behind_f, whole(chunk_f))
    full_b = (block_b, behind_b[0], y_b)
    piece_3 = own(full_b, 0, core_b[0], 0, 3)
    piece_4 = own(gate(full_b, piece_3), 1, core_b[1], 0, 4)
    recv_2 = relay(jnp.concatenate([piece_2[cut:], piece_3, piece_4]))
    block_f = gate(block_f, piece_4, recv_1)
    core_f = over_core(block_f, behind_f, y_f, (0, 2))
    core_7 = over_core(block_f, behind_f, y_f, (2, 1))
    full_f = (block_f, behind_f[0], y_f)
    piece_5 = passed(full_f, 0, core_f, 0, wide_a, 0)
    piece_6 = passed(gate(full_f, piece_5), 1, core_f, 1, wide_b, 0)
    piece_7 = passed(gate(full_f, piece_6), 2, core_7, 0, wide_b, 2 * tokens)
    rest = tokens - cut
    pieces = [
        (recv_0, (0, 0)),
        (recv_1[:rest], (cut, 0)),
        (recv_1[rest : rest + tokens], (0, WIDTH)),
        (recv_1[rest + tokens :], (0, 2 * WIDTH)),
        (piece_5, (0, 5 * WIDTH)),
        (piece_6, (0, 6 * WIDTH)),
        (piece_7, (0, 7 * WIDTH)),
    ]
    out = assemble(None, pieces, queries.shape, LIGHT)
    recv_2 = gate(recv_2, out)
    out = lax.dynamic_update_slice(out, recv_2[:rest], (cut, 2 * WIDTH))
    last = jnp.concatenate([recv_2[rest : rest + tokens], recv_2[rest + tokens :]], axis=1)
    return lax.dynamic_update_slice(out, last, (0, 3 * WIDTH))[None]


def solution(mesh):
    in_specs = (
        P("section", "ctx", None),
        P("section", "ctx", None),
        P("section", "ctx", None),
        P("section", "ctx", None),
        P("section", "ctx"),
    )
    out_specs = P("section", "ctx", None)
    return jax.shard_map(local, mesh=mesh, in_specs=in_specs, out_specs=out_specs, check_vma=False)
```

```python
import functools
import math

import jax
import jax.numpy as jnp
from jax import lax
from jax.experimental import pallas as pl
from jax.experimental.pallas import tpu as pltpu
from jax.sharding import PartitionSpec as P

HQ = 64
KVH = 8
HD = 128
WINDOW = 8
REPEAT = HQ // KVH
PAIR = 2 * HD
WIDTH = REPEAT * HD
SEG_ROWS = 16
PENALTY = float(2**20)
LOG2_SCALE = HD**-0.5 * math.log2(math.e)
LIGHT = pl.CostEstimate(flops=1, bytes_accessed=1, transcendentals=0)
HEAVY = pl.CostEstimate(flops=10**11, bytes_accessed=10**6, transcendentals=0)
SLOTS = (
    (7, 3, 5, 1, 4, 6, 2, 0),
    (7, 3, 5, 1, 2, 4, 0, 6),
    (7, 3, 1, 5, 4, 2, 6, 0),
    (7, 3, 1, 5, 2, 0, 4, 6),
)


def gate(value, *ahead):
    return lax.optimization_barrier((value, ahead))[0]


def exchange(value, axis, bit):
    return lax.ppermute(value, axis, [(i, i ^ bit) for i in range(lax.axis_size(axis))])


def from_groups_behind(value, groups):
    size = lax.axis_size("ctx")
    pairs = [(i, i + 4 * groups) for i in range(size - 4 * groups)]
    if not {a for a, _ in pairs} & {b for _, b in pairs}:
        pairs = pairs + [(b, a) for a, b in pairs]
    return lax.ppermute(value, "ctx", pairs)


def gather_behind(block):
    return from_groups_behind(block, 1), from_groups_behind(block, 2)


def join_kernel(bit, column, *refs):
    *parts, own, two, out = refs
    width = out.shape[1]
    row = 0
    for part in parts:
        start = column if part.shape[1] > width else 0
        out[row : row + part.shape[0], :] = part[:, start : start + width]
        row += part.shape[0]
    first = (lax.axis_index("ctx") // bit) % 2 == 0

    @pl.when(first)
    def _():
        out[row:, :] = own[:, column : column + width]

    @pl.when(jnp.logical_not(first))
    def _():
        out[row:, :] = two[:, column : column + width]


def join(parts, own, two, bit, chunk):
    first, size = chunk
    rows = sum(part.shape[0] for part in parts) + own.shape[0]
    vmem = pl.BlockSpec(memory_space=pltpu.VMEM)
    return pl.pallas_call(
        functools.partial(join_kernel, bit, first * PAIR),
        in_specs=[vmem] * (len(parts) + 2),
        out_specs=vmem,
        out_shape=jax.ShapeDtypeStruct((rows, size * PAIR), jnp.bfloat16),
        cost_estimate=LIGHT,
        compiler_params=pltpu.CompilerParams(vmem_limit_bytes=12 * 2**20),
        name="join",
    )(*parts, own, two)


def over_y(block, behind, chunk):
    one, two = behind
    return exchange(join([one], block, two, 2, chunk), "ctx", 2)


def over_core(block, behind, mates, chunk):
    one, two = behind
    return exchange(join([one, mates], block, two, 1, chunk), "ctx", 1)


def fill_block(out, tokens, chunk, keys, values, seg):
    first, size = chunk
    for n in range(size):
        source = slice((first + n) * HD, (first + n + 1) * HD)
        out[:tokens, n * PAIR : n * PAIR + HD] = keys[:, source]
        out[:tokens, n * PAIR + HD : (n + 1) * PAIR] = values[:, source]
    out[tokens:, :] = jnp.zeros((out.shape[0] - tokens, size * PAIR), jnp.bfloat16)
    row = seg[...].astype(jnp.float32).astype(jnp.bfloat16)
    for n in range(size):
        out[tokens : tokens + 1, n * PAIR : n * PAIR + tokens] = row


def fold_places(rows, size):
    per_row = WIDTH // PAIR
    tiles = [(n, r) for n in range(size) for r in range(rows // SEG_ROWS)]
    return [
        (r * SEG_ROWS, n * PAIR, t // per_row * SEG_ROWS, t % per_row * PAIR)
        for t, (n, r) in enumerate(tiles)
    ]


def pack_first_kernel(chunks, passed, query_head, queries, keys_in, values_in, seg_in, *refs):
    *blocks, out, block, keys, values, seg, sems = refs
    tokens = queries.shape[0]
    copies = [
        pltpu.make_async_copy(source, target, sems.at[n])
        for n, (source, target) in enumerate(
            (
                (keys_in, keys),
                (values_in, values),
                (seg_in, seg),
                (queries.at[:, pl.ds(query_head * WIDTH, WIDTH)], out.at[pl.ds(0, tokens)]),
            )
        )
    ]
    for copy in copies:
        copy.start()
    for copy in copies[:3]:
        copy.wait()
    for target, chunk in zip(blocks, chunks):
        fill_block(target, tokens, chunk, keys, values, seg)
    fill_block(block, tokens, passed, keys, values, seg)
    for row, column, to_row, to_column in fold_places(block.shape[0], passed[1]):
        out[tokens + to_row : tokens + to_row + SEG_ROWS, to_column : to_column + PAIR] = block[
            row : row + SEG_ROWS, column : column + PAIR
        ]
    copies[3].wait()


def pack_first(queries, keys, values, segments, chunks, passed):
    tokens = queries.shape[0]
    block = lambda chunk: (tokens + SEG_ROWS, chunk[1] * PAIR)
    folded = max(place[2] for place in fold_places(tokens + SEG_ROWS, passed[1])) + SEG_ROWS
    shapes = [block(chunk) for chunk in chunks] + [(tokens + folded, WIDTH)]
    vmem = pl.BlockSpec(memory_space=pltpu.VMEM)
    return pl.pallas_call(
        functools.partial(pack_first_kernel, chunks, passed, passed[0]),
        in_specs=[pl.BlockSpec(memory_space=pltpu.HBM)] * 4,
        out_specs=[vmem] * len(shapes),
        out_shape=[jax.ShapeDtypeStruct(shape, jnp.bfloat16) for shape in shapes],
        scratch_shapes=[
            pltpu.VMEM(block(passed), jnp.bfloat16),
            pltpu.VMEM(keys.shape, jnp.bfloat16),
            pltpu.VMEM(values.shape, jnp.bfloat16),
            pltpu.VMEM(segments.shape, segments.dtype),
            pltpu.SemaphoreType.DMA((4,)),
        ],
        cost_estimate=LIGHT,
        compiler_params=pltpu.CompilerParams(vmem_limit_bytes=56 * 2**20),
        name="pack_first",
    )(queries, keys, values, segments)


def pack_wide_kernel(parts, queries, stream, out, sems):
    tokens = queries.shape[0]
    copies = [
        pltpu.make_async_copy(
            (queries, stream)[m].at[:, pl.ds(head * WIDTH, WIDTH)],
            out.at[pl.ds(n * tokens, tokens)],
            sems.at[n],
        )
        for n, (m, head) in enumerate(parts)
    ]
    for copy in copies:
        copy.start()
    for copy in copies:
        copy.wait()


def pack_wide(queries, stream, parts):
    return pl.pallas_call(
        functools.partial(pack_wide_kernel, parts),
        in_specs=[pl.BlockSpec(memory_space=pltpu.HBM)] * 2,
        out_specs=pl.BlockSpec(memory_space=pltpu.VMEM),
        out_shape=jax.ShapeDtypeStruct((len(parts) * queries.shape[0], WIDTH), jnp.bfloat16),
        scratch_shapes=[pltpu.SemaphoreType.DMA((len(parts),))],
        cost_estimate=LIGHT,
        compiler_params=pltpu.CompilerParams(vmem_limit_bytes=56 * 2**20),
        name="pack_wide",
    )(queries, stream)


def unfold_kernel(base, size, wide, out):
    for row, column, at_row, at_column in fold_places(out.shape[0], size):
        out[row : row + SEG_ROWS, column : column + PAIR] = wide[
            base + at_row : base + at_row + SEG_ROWS, at_column : at_column + PAIR
        ]


def unfold(wide, base, tokens, chunk):
    vmem = pl.BlockSpec(memory_space=pltpu.VMEM)
    return pl.pallas_call(
        functools.partial(unfold_kernel, base, chunk[1]),
        in_specs=[vmem],
        out_specs=vmem,
        out_shape=jax.ShapeDtypeStruct((tokens + SEG_ROWS, chunk[1] * PAIR), jnp.bfloat16),
        cost_estimate=LIGHT,
        compiler_params=pltpu.CompilerParams(vmem_limit_bytes=8 * 2**20),
        name="unfold",
    )(wide)


def attend_kernel(tokens, column, query_row, stream_row, *refs):
    blocks, (query_in, stream_in, out) = refs[:WINDOW], refs[WINDOW : WINDOW + 3]
    keys, values, bias, extra, segs_ref, query, stream, sems = refs[WINDOW + 3 :]
    window = tokens * WINDOW
    index = lax.axis_index("ctx")
    place = index % 4
    slots = [
        jnp.where(place < 2, jnp.where(place == 0, a, b), jnp.where(place == 2, c, d))
        for a, b, c, d in zip(*SLOTS)
    ]
    copies = [
        pltpu.make_async_copy(
            source.at[pl.ds(row, tokens), pl.ds(column, WIDTH)], target, sems.at[n]
        )
        for n, (source, row, target) in enumerate(
            ((query_in, query_row, query), (stream_in, stream_row, stream))
        )
    ]

    for copy in copies:
        copy.start()
    for slot, block in zip(slots, blocks):
        row = block[tokens : tokens + 1, :].astype(jnp.float32)
        segs_ref[pl.ds(slot, 1), :] = jnp.where(slot + index >= WINDOW - 1, row, -1.0)
    segs = segs_ref[...]
    own_row = segs[WINDOW - 1 :, :tokens]
    seg_zero = segs[WINDOW - 1 :, 0:1]
    own_column = segs.T[:tokens, WINDOW - 1 :]
    before = jnp.sum(jnp.where(segs[: WINDOW - 1, :tokens] != seg_zero, 1.0, 0.0))
    lane = lax.broadcasted_iota(jnp.int32, (tokens, HD), 1)
    extra[...] = jnp.where(
        lane == 0,
        jnp.where(own_column == seg_zero, 0.0, -PENALTY),
        jnp.where(lane == 1, -PENALTY, 0.0),
    ).astype(jnp.bfloat16)
    row_id = lax.broadcasted_iota(jnp.int32, (tokens, tokens), 0)
    column_id = lax.broadcasted_iota(jnp.int32, (tokens, tokens), 1)
    tail = bias.shape[1]
    bias[:, : tail - tokens] = jnp.zeros((tokens, tail - tokens), jnp.float32)
    bias[:, tail - tokens :] = jnp.where(
        (own_column == own_row) & (column_id <= row_id), 0.0, -PENALTY
    )
    key_row = lax.broadcasted_iota(jnp.int32, (window, HD), 0)
    key_lane = lax.broadcasted_iota(jnp.int32, (window, HD), 1)
    keys[:, HD:] = jnp.where(
        ((key_lane == 0) & (key_row < window - tokens))
        | ((key_lane == 1) & (key_row.astype(jnp.float32) < before)),
        1.0,
        0.0,
    ).astype(jnp.bfloat16)
    values[:, HD:] = jnp.ones((window, HD), jnp.bfloat16)

    for copy in copies:
        copy.wait()

    for slot, block in zip(slots, blocks):
        rows = pl.ds(pl.multiple_of(slot * tokens, tokens), tokens)
        keys[rows, :HD] = block[:tokens, :HD]
        values[rows, :HD] = block[:tokens, HD:]

    def columns(head):
        return slice(head * HD, (head + 1) * HD)

    def score(head):
        marks = extra[...]
        rows = jnp.concatenate(
            [jnp.concatenate([query[:, columns(h)], marks], axis=1) for h in (head, head + 1)],
            axis=0,
        )
        scores = lax.dot_general(
            rows, keys[...], (((1,), (1,)), ((), ())), preferred_element_type=jnp.float32
        )
        own = scores[:, window - tail :] + jnp.concatenate([bias[...]] * 2, axis=0)
        return jnp.concatenate([scores[:, : window - tail], own], axis=1)

    def finish(head, scores):
        top = jnp.max(scores, axis=1, keepdims=True)
        weights = jnp.exp2((scores - top) * LOG2_SCALE).astype(jnp.bfloat16)
        sums = jnp.dot(weights, values[...], preferred_element_type=jnp.float32)
        attended = sums[:, :HD] / sums[:, HD:]
        for n, h in enumerate((head, head + 1)):
            out[:, columns(h)] = (
                attended[n * tokens : (n + 1) * tokens]
                + stream[:, columns(h)].astype(jnp.float32)
            ).astype(jnp.bfloat16)

    scores = score(0)
    for head in range(0, REPEAT, 2):
        later = score(head + 2) if head + 2 < REPEAT else None
        finish(head, scores)
        scores = later


def attend(blocks, queries, stream, column, query_row, stream_row, cost):
    rows = blocks[0][0].shape[0]
    tokens = rows - SEG_ROWS
    window = tokens * WINDOW
    places = [(block, part, n) for block, part in blocks for n in range(block.shape[0] // rows)]
    return pl.pallas_call(
        functools.partial(attend_kernel, tokens, column, query_row, stream_row),
        grid=(1,),
        in_specs=[
            pl.BlockSpec((rows, PAIR), lambda i, part=part, n=n: (n, part)) for _, part, n in places
        ]
        + [pl.BlockSpec(memory_space=pl.ANY)] * 2,
        out_specs=pl.BlockSpec((tokens, WIDTH), lambda i: (0, 0)),
        out_shape=jax.ShapeDtypeStruct((tokens, WIDTH), jnp.bfloat16),
        scratch_shapes=[
            pltpu.VMEM((window, PAIR), jnp.bfloat16),
            pltpu.VMEM((window, PAIR), jnp.bfloat16),
            pltpu.VMEM((tokens, PAIR), jnp.float32),
            pltpu.VMEM((tokens, HD), jnp.bfloat16),
            pltpu.VMEM((WINDOW, PAIR), jnp.float32),
            pltpu.VMEM((tokens, WIDTH), jnp.bfloat16),
            pltpu.VMEM((tokens, WIDTH), jnp.bfloat16),
            pltpu.SemaphoreType.DMA((2,)),
        ],
        compiler_params=pltpu.CompilerParams(vmem_limit_bytes=16 * 2**20),
        cost_estimate=cost,
        name="attend",
    )(*[block for block, _, _ in places], queries, stream)


def assemble_kernel(places, *refs):
    *pieces, out, sems = refs
    copies = [
        pltpu.make_async_copy(
            piece, out.at[pl.ds(row, piece.shape[0]), pl.ds(column, piece.shape[1])], sems.at[n]
        )
        for n, (piece, (row, column)) in enumerate(zip(pieces[-len(places) :], places))
    ]
    for copy in copies:
        copy.start()
    for copy in copies:
        copy.wait()


def assemble(out, pieces, shape, cost):
    places = [place for _, place in pieces]
    given = [] if out is None else [out]
    return pl.pallas_call(
        functools.partial(assemble_kernel, places),
        in_specs=[pl.BlockSpec(memory_space=pl.ANY)] * len(given)
        + [pl.BlockSpec(memory_space=pltpu.VMEM)] * len(pieces),
        out_specs=pl.BlockSpec(memory_space=pl.ANY),
        out_shape=jax.ShapeDtypeStruct(shape, jnp.bfloat16),
        scratch_shapes=[pltpu.SemaphoreType.DMA((len(pieces),))],
        input_output_aliases={0: 0} if given else {},
        cost_estimate=cost,
        compiler_params=pltpu.CompilerParams(vmem_limit_bytes=8 * 2**20),
        name="assemble",
    )(*given, *[piece for piece, _ in pieces])


def local(stream, queries, keys, values, segments):
    stream, queries, keys, values = stream[0], queries[0], keys[0], values[0]
    segments = segments.reshape(1, -1)
    tokens = queries.shape[0]
    relay = lambda value: exchange(value, "section", 1)
    def own(full, n, core, at, head):
        at = [(part, n) for part in full] + [(core, at)]
        return attend(at, queries, stream, head * WIDTH, 0, 0, LIGHT)

    def passed(full, n, core, at, q, q_row, s_row):
        at = [(part, n) for part in full] + [(core, at)]
        return attend(at, q, wide_b, 0, q_row, s_row, LIGHT)

    chunk_a, chunk_b, chunk_f = (0, 3), (3, 2), (5, 3)
    cut = 3 * tokens // 4
    whole = lambda chunk: (0, chunk[1])
    block_a, block_b, wide_a = pack_first(queries, keys, values, segments, (chunk_a, chunk_b), chunk_f)
    wide_a = relay(wide_a)
    behind_a = gather_behind(block_a)
    wide_b = pack_wide(gate(queries, block_a), stream, ((1, 5), (0, 6), (1, 6), (0, 7), (1, 7)))
    wide_b, behind_a = relay(wide_b), gate(behind_a, wide_a)
    block_f = unfold(wide_a, tokens, tokens, chunk_f)
    behind_b = gather_behind(gate(block_b, behind_a))
    y_a = over_y(block_a, behind_a, whole(chunk_a))
    behind_f = gather_behind(gate(block_f, behind_b, y_a))
    y_b = over_y(gate(block_b, y_a), behind_b, whole(chunk_b))
    block_a = gate(block_a, behind_b)
    core_a = over_core(block_a, behind_a, y_a, (0, 2))
    core_2 = over_core(block_a, behind_a, y_a, (2, 1))
    full_a = (block_a, behind_a[0], y_a)
    piece_0 = own(full_a, 0, core_a, 0, 0)
    recv_0 = relay(piece_0[:cut])
    piece_1 = own(gate(full_a, piece_0), 1, core_a, 1, 1)
    piece_2 = own(gate(full_a, piece_1), 2, core_2, 0, 2)
    recv_1 = relay(jnp.concatenate([piece_0[cut:], piece_1, piece_2[:cut]]))
    block_b, block_f = gate((block_b, block_f), behind_f, y_b, recv_0, piece_2, wide_b)
    core_b = [over_core(block_b, behind_b, y_b, (n, 1)) for n in range(chunk_b[1])]
    y_f = over_y(block_f, behind_f, whole(chunk_f))
    full_b = (block_b, behind_b[0], y_b)
    piece_3 = own(full_b, 0, core_b[0], 0, 3)
    piece_4 = own(gate(full_b, piece_3), 1, core_b[1], 0, 4)
    recv_2 = relay(jnp.concatenate([piece_2[cut:], piece_3, piece_4]))
    block_f = gate(block_f, piece_4, recv_1)
    core_f = over_core(block_f, behind_f, y_f, (0, 2))
    rest = tokens - cut
    early = [
        (recv_0, (0, 0)),
        (recv_1[:rest], (cut, 0)),
        (recv_1[rest : rest + tokens], (0, WIDTH)),
        (recv_1[rest + tokens :], (0, 2 * WIDTH)),
    ]
    out = assemble(None, early, queries.shape, LIGHT)
    core_7 = over_core(gate(block_f, out), behind_f, y_f, (2, 1))
    full_f = (block_f, behind_f[0], y_f)
    piece_5 = passed(full_f, 0, core_f, 0, wide_a, 0, 0)
    piece_6 = passed(gate(full_f, piece_5), 1, core_f, 1, wide_b, tokens, 2 * tokens)
    piece_7 = passed(gate(full_f, piece_6), 2, core_7, 0, wide_b, 3 * tokens, 4 * tokens)
    recv_2 = gate(recv_2, piece_7)
    late = [
        (piece_5, (0, 5 * WIDTH)),
        (piece_6, (0, 6 * WIDTH)),
        (piece_7, (0, 7 * WIDTH)),
        (recv_2[:rest], (cut, 2 * WIDTH)),
        (recv_2[rest : rest + tokens], (0, 3 * WIDTH)),
        (recv_2[rest + tokens :], (0, 4 * WIDTH)),
    ]
    return assemble(out, late, queries.shape, LIGHT)[None]


def solution(mesh):
    in_specs = (
        P("section", "ctx", None),
        P("section", "ctx", None),
        P("section", "ctx", None),
        P("section", "ctx", None),
        P("section", "ctx"),
    )
    out_specs = P("section", "ctx", None)
    return jax.shard_map(local, mesh=mesh, in_specs=in_specs, out_specs=out_specs, check_vma=False)
```

```python
import functools
import math

import jax
import jax.numpy as jnp
from jax import lax
from jax.experimental import pallas as pl
from jax.experimental.pallas import tpu as pltpu
from jax.sharding import PartitionSpec as P

HQ = 64
KVH = 8
HD = 128
WINDOW = 8
REPEAT = HQ // KVH
PAIR = 2 * HD
WIDTH = REPEAT * HD
SEG_ROWS = 16
PENALTY = float(2**20)
LOG2_SCALE = HD**-0.5 * math.log2(math.e)
LIGHT = pl.CostEstimate(flops=1, bytes_accessed=1, transcendentals=0)
HEAVY = pl.CostEstimate(flops=10**11, bytes_accessed=10**6, transcendentals=0)
SLOTS = (
    (7, 3, 5, 1, 4, 6, 2, 0),
    (7, 3, 5, 1, 2, 4, 0, 6),
    (7, 3, 1, 5, 4, 2, 6, 0),
    (7, 3, 1, 5, 2, 0, 4, 6),
)


def gate(value, *ahead):
    return lax.optimization_barrier((value, ahead))[0]


def exchange(value, axis, bit):
    return lax.ppermute(value, axis, [(i, i ^ bit) for i in range(lax.axis_size(axis))])


def from_groups_behind(value, groups):
    size = lax.axis_size("ctx")
    pairs = [(i, i + 4 * groups) for i in range(size - 4 * groups)]
    if not {a for a, _ in pairs} & {b for _, b in pairs}:
        pairs = pairs + [(b, a) for a, b in pairs]
    return lax.ppermute(value, "ctx", pairs)


def gather_behind(block):
    return from_groups_behind(block, 1), from_groups_behind(block, 2)


def join_kernel(bit, column, *refs):
    *parts, own, two, out = refs
    width = out.shape[1]
    row = 0
    for part in parts:
        start = column if part.shape[1] > width else 0
        out[row : row + part.shape[0], :] = part[:, start : start + width]
        row += part.shape[0]
    first = (lax.axis_index("ctx") // bit) % 2 == 0

    @pl.when(first)
    def _():
        out[row:, :] = own[:, column : column + width]

    @pl.when(jnp.logical_not(first))
    def _():
        out[row:, :] = two[:, column : column + width]


def join(parts, own, two, bit, chunk):
    first, size = chunk
    rows = sum(part.shape[0] for part in parts) + own.shape[0]
    vmem = pl.BlockSpec(memory_space=pltpu.VMEM)
    return pl.pallas_call(
        functools.partial(join_kernel, bit, first * PAIR),
        in_specs=[vmem] * (len(parts) + 2),
        out_specs=vmem,
        out_shape=jax.ShapeDtypeStruct((rows, size * PAIR), jnp.bfloat16),
        cost_estimate=LIGHT,
        compiler_params=pltpu.CompilerParams(vmem_limit_bytes=12 * 2**20),
        name="join",
    )(*parts, own, two)


def over_y(block, behind, chunk):
    one, two = behind
    return exchange(join([one], block, two, 2, chunk), "ctx", 2)


def over_core(block, behind, mates, chunk):
    one, two = behind
    return exchange(join([one, mates], block, two, 1, chunk), "ctx", 1)


def fill_block(out, tokens, chunk, keys, values, seg):
    first, size = chunk
    for n in range(size):
        source = slice((first + n) * HD, (first + n + 1) * HD)
        out[:tokens, n * PAIR : n * PAIR + HD] = keys[:, source]
        out[:tokens, n * PAIR + HD : (n + 1) * PAIR] = values[:, source]
    out[tokens:, :] = jnp.zeros((out.shape[0] - tokens, size * PAIR), jnp.bfloat16)
    row = seg[...].astype(jnp.float32).astype(jnp.bfloat16)
    for n in range(size):
        out[tokens : tokens + 1, n * PAIR : n * PAIR + tokens] = row


def fold_places(rows, size):
    per_row = WIDTH // PAIR
    tiles = [(n, r) for n in range(size) for r in range(rows // SEG_ROWS)]
    return [
        (r * SEG_ROWS, n * PAIR, t // per_row * SEG_ROWS, t % per_row * PAIR)
        for t, (n, r) in enumerate(tiles)
    ]


def pack_first_kernel(chunks, passed, keys_in, values_in, seg_in, *refs):
    *blocks, out, block, keys, values, seg, sems = refs
    tokens = keys_in.shape[0]
    copies = [
        pltpu.make_async_copy(source, target, sems.at[n])
        for n, (source, target) in enumerate(
            (
                (keys_in, keys),
                (values_in, values),
                (seg_in, seg),
            )
        )
    ]
    for copy in copies:
        copy.start()
    for copy in copies:
        copy.wait()
    for target, chunk in zip(blocks, chunks):
        fill_block(target, tokens, chunk, keys, values, seg)
    fill_block(block, tokens, passed, keys, values, seg)
    for row, column, to_row, to_column in fold_places(block.shape[0], passed[1]):
        out[to_row : to_row + SEG_ROWS, to_column : to_column + PAIR] = block[
            row : row + SEG_ROWS, column : column + PAIR
        ]


def pack_first(keys, values, segments, chunks, passed):
    tokens = keys.shape[0]
    block = lambda chunk: (tokens + SEG_ROWS, chunk[1] * PAIR)
    folded = max(place[2] for place in fold_places(tokens + SEG_ROWS, passed[1])) + SEG_ROWS
    shapes = [block(chunk) for chunk in chunks] + [(folded, WIDTH)]
    vmem = pl.BlockSpec(memory_space=pltpu.VMEM)
    return pl.pallas_call(
        functools.partial(pack_first_kernel, chunks, passed),
        in_specs=[pl.BlockSpec(memory_space=pltpu.HBM)] * 3,
        out_specs=[vmem] * len(shapes),
        out_shape=[jax.ShapeDtypeStruct(shape, jnp.bfloat16) for shape in shapes],
        scratch_shapes=[
            pltpu.VMEM(block(passed), jnp.bfloat16),
            pltpu.VMEM(keys.shape, jnp.bfloat16),
            pltpu.VMEM(values.shape, jnp.bfloat16),
            pltpu.VMEM(segments.shape, segments.dtype),
            pltpu.SemaphoreType.DMA((3,)),
        ],
        cost_estimate=LIGHT,
        compiler_params=pltpu.CompilerParams(vmem_limit_bytes=56 * 2**20),
        name="pack_first",
    )(keys, values, segments)


def pack_wide_kernel(parts, queries, stream, out, sems):
    tokens = queries.shape[0]
    copies = [
        pltpu.make_async_copy(
            (queries, stream)[m].at[:, pl.ds(head * WIDTH, WIDTH)],
            out.at[pl.ds(n * tokens, tokens)],
            sems.at[n],
        )
        for n, (m, head) in enumerate(parts)
    ]
    for copy in copies:
        copy.start()
    for copy in copies:
        copy.wait()


def pack_wide(queries, stream, parts):
    return pl.pallas_call(
        functools.partial(pack_wide_kernel, parts),
        in_specs=[pl.BlockSpec(memory_space=pltpu.HBM)] * 2,
        out_specs=pl.BlockSpec(memory_space=pltpu.VMEM),
        out_shape=jax.ShapeDtypeStruct((len(parts) * queries.shape[0], WIDTH), jnp.bfloat16),
        scratch_shapes=[pltpu.SemaphoreType.DMA((len(parts),))],
        cost_estimate=LIGHT,
        compiler_params=pltpu.CompilerParams(vmem_limit_bytes=56 * 2**20),
        name="pack_wide",
    )(queries, stream)


def unfold_kernel(base, size, wide, out):
    for row, column, at_row, at_column in fold_places(out.shape[0], size):
        out[row : row + SEG_ROWS, column : column + PAIR] = wide[
            base + at_row : base + at_row + SEG_ROWS, at_column : at_column + PAIR
        ]


def unfold(wide, base, tokens, chunk):
    vmem = pl.BlockSpec(memory_space=pltpu.VMEM)
    return pl.pallas_call(
        functools.partial(unfold_kernel, base, chunk[1]),
        in_specs=[vmem],
        out_specs=vmem,
        out_shape=jax.ShapeDtypeStruct((tokens + SEG_ROWS, chunk[1] * PAIR), jnp.bfloat16),
        cost_estimate=LIGHT,
        compiler_params=pltpu.CompilerParams(vmem_limit_bytes=8 * 2**20),
        name="unfold",
    )(wide)


def attend_kernel(tokens, column, query_row, stream_row, *refs):
    blocks, (query_in, stream_in, out) = refs[:WINDOW], refs[WINDOW : WINDOW + 3]
    keys, values, bias, extra, segs_ref, query, stream, sems = refs[WINDOW + 3 :]
    window = tokens * WINDOW
    index = lax.axis_index("ctx")
    place = index % 4
    slots = [
        jnp.where(place < 2, jnp.where(place == 0, a, b), jnp.where(place == 2, c, d))
        for a, b, c, d in zip(*SLOTS)
    ]
    copies = [
        pltpu.make_async_copy(
            source.at[pl.ds(row, tokens), pl.ds(column, WIDTH)], target, sems.at[n]
        )
        for n, (source, row, target) in enumerate(
            ((query_in, query_row, query), (stream_in, stream_row, stream))
        )
    ]

    for copy in copies:
        copy.start()
    for slot, block in zip(slots, blocks):
        row = block[tokens : tokens + 1, :].astype(jnp.float32)
        segs_ref[pl.ds(slot, 1), :] = jnp.where(slot + index >= WINDOW - 1, row, -1.0)
    segs = segs_ref[...]
    own_row = segs[WINDOW - 1 :, :tokens]
    seg_zero = segs[WINDOW - 1 :, 0:1]
    own_column = segs.T[:tokens, WINDOW - 1 :]
    before = jnp.sum(jnp.where(segs[: WINDOW - 1, :tokens] != seg_zero, 1.0, 0.0))
    lane = lax.broadcasted_iota(jnp.int32, (tokens, HD), 1)
    extra[...] = jnp.where(
        lane == 0,
        jnp.where(own_column == seg_zero, 0.0, -PENALTY),
        jnp.where(lane == 1, -PENALTY, 0.0),
    ).astype(jnp.bfloat16)
    row_id = lax.broadcasted_iota(jnp.int32, (tokens, tokens), 0)
    column_id = lax.broadcasted_iota(jnp.int32, (tokens, tokens), 1)
    tail = bias.shape[1]
    bias[:, : tail - tokens] = jnp.zeros((tokens, tail - tokens), jnp.float32)
    bias[:, tail - tokens :] = jnp.where(
        (own_column == own_row) & (column_id <= row_id), 0.0, -PENALTY
    )
    key_row = lax.broadcasted_iota(jnp.int32, (window, HD), 0)
    key_lane = lax.broadcasted_iota(jnp.int32, (window, HD), 1)
    keys[:, HD:] = jnp.where(
        ((key_lane == 0) & (key_row < window - tokens))
        | ((key_lane == 1) & (key_row.astype(jnp.float32) < before)),
        1.0,
        0.0,
    ).astype(jnp.bfloat16)
    values[:, HD:] = jnp.ones((window, HD), jnp.bfloat16)

    for copy in copies:
        copy.wait()

    for slot, block in zip(slots, blocks):
        rows = pl.ds(pl.multiple_of(slot * tokens, tokens), tokens)
        keys[rows, :HD] = block[:tokens, :HD]
        values[rows, :HD] = block[:tokens, HD:]

    def columns(head):
        return slice(head * HD, (head + 1) * HD)

    def score(head):
        marks = extra[...]
        rows = jnp.concatenate(
            [jnp.concatenate([query[:, columns(h)], marks], axis=1) for h in (head, head + 1)],
            axis=0,
        )
        scores = lax.dot_general(
            rows, keys[...], (((1,), (1,)), ((), ())), preferred_element_type=jnp.float32
        )
        own = scores[:, window - tail :] + jnp.concatenate([bias[...]] * 2, axis=0)
        return jnp.concatenate([scores[:, : window - tail], own], axis=1)

    def finish(head, scores):
        top = jnp.max(scores, axis=1, keepdims=True)
        weights = jnp.exp2((scores - top) * LOG2_SCALE).astype(jnp.bfloat16)
        sums = jnp.dot(weights, values[...], preferred_element_type=jnp.float32)
        attended = sums[:, :HD] / sums[:, HD:]
        for n, h in enumerate((head, head + 1)):
            out[:, columns(h)] = (
                attended[n * tokens : (n + 1) * tokens]
                + stream[:, columns(h)].astype(jnp.float32)
            ).astype(jnp.bfloat16)

    scores = score(0)
    for head in range(0, REPEAT, 2):
        later = score(head + 2) if head + 2 < REPEAT else None
        finish(head, scores)
        scores = later


def attend(blocks, queries, stream, column, query_row, stream_row, cost):
    rows = blocks[0][0].shape[0]
    tokens = rows - SEG_ROWS
    window = tokens * WINDOW
    places = [(block, part, n) for block, part in blocks for n in range(block.shape[0] // rows)]
    return pl.pallas_call(
        functools.partial(attend_kernel, tokens, column, query_row, stream_row),
        grid=(1,),
        in_specs=[
            pl.BlockSpec((rows, PAIR), lambda i, part=part, n=n: (n, part)) for _, part, n in places
        ]
        + [pl.BlockSpec(memory_space=pl.ANY)] * 2,
        out_specs=pl.BlockSpec((tokens, WIDTH), lambda i: (0, 0)),
        out_shape=jax.ShapeDtypeStruct((tokens, WIDTH), jnp.bfloat16),
        scratch_shapes=[
            pltpu.VMEM((window, PAIR), jnp.bfloat16),
            pltpu.VMEM((window, PAIR), jnp.bfloat16),
            pltpu.VMEM((tokens, PAIR), jnp.float32),
            pltpu.VMEM((tokens, HD), jnp.bfloat16),
            pltpu.VMEM((WINDOW, PAIR), jnp.float32),
            pltpu.VMEM((tokens, WIDTH), jnp.bfloat16),
            pltpu.VMEM((tokens, WIDTH), jnp.bfloat16),
            pltpu.SemaphoreType.DMA((2,)),
        ],
        compiler_params=pltpu.CompilerParams(vmem_limit_bytes=16 * 2**20),
        cost_estimate=cost,
        name="attend",
    )(*[block for block, _, _ in places], queries, stream)


def assemble_kernel(places, *refs):
    *pieces, out, sems = refs
    copies = [
        pltpu.make_async_copy(
            piece, out.at[pl.ds(row, piece.shape[0]), pl.ds(column, piece.shape[1])], sems.at[n]
        )
        for n, (piece, (row, column)) in enumerate(zip(pieces[-len(places) :], places))
    ]
    for copy in copies:
        copy.start()
    for copy in copies:
        copy.wait()


def assemble(out, pieces, shape, cost):
    places = [place for _, place in pieces]
    given = [] if out is None else [out]
    return pl.pallas_call(
        functools.partial(assemble_kernel, places),
        in_specs=[pl.BlockSpec(memory_space=pl.ANY)] * len(given)
        + [pl.BlockSpec(memory_space=pltpu.VMEM)] * len(pieces),
        out_specs=pl.BlockSpec(memory_space=pl.ANY),
        out_shape=jax.ShapeDtypeStruct(shape, jnp.bfloat16),
        scratch_shapes=[pltpu.SemaphoreType.DMA((len(pieces),))],
        input_output_aliases={0: 0} if given else {},
        cost_estimate=cost,
        compiler_params=pltpu.CompilerParams(vmem_limit_bytes=8 * 2**20),
        name="assemble",
    )(*given, *[piece for piece, _ in pieces])


def local(stream, queries, keys, values, segments):
    stream, queries, keys, values = stream[0], queries[0], keys[0], values[0]
    segments = segments.reshape(1, -1)
    tokens = queries.shape[0]
    relay = lambda value: exchange(value, "section", 1)
    def own(full, n, core, at, head):
        at = [(part, n) for part in full] + [(core, at)]
        return attend(at, queries, stream, head * WIDTH, 0, 0, LIGHT)

    def passed(full, n, core, at, q, q_row, s_row):
        at = [(part, n) for part in full] + [(core, at)]
        return attend(at, q, wide_b, 0, q_row, s_row, LIGHT)

    chunk_a, chunk_b, chunk_f = (0, 3), (3, 2), (5, 3)
    cut = 3 * tokens // 4
    whole = lambda chunk: (0, chunk[1])
    query_5 = queries[:, 5 * WIDTH : 6 * WIDTH]
    keys = gate(keys, query_5)
    query_5 = relay(query_5)
    block_a, block_b, wide_a = pack_first(keys, values, segments, (chunk_a, chunk_b), chunk_f)
    wide_a = relay(wide_a)
    behind_a = gather_behind(block_a)
    wide_b = pack_wide(gate(queries, block_a), stream, ((1, 5), (0, 6), (1, 6), (0, 7), (1, 7)))
    wide_b, behind_a = relay(wide_b), gate(behind_a, wide_a, query_5)
    block_f = unfold(wide_a, 0, tokens, chunk_f)
    behind_b = gather_behind(gate(block_b, behind_a))
    y_a = over_y(block_a, behind_a, whole(chunk_a))
    behind_f = gather_behind(gate(block_f, behind_b, y_a))
    y_b = over_y(gate(block_b, y_a), behind_b, whole(chunk_b))
    block_a = gate(block_a, behind_b)
    core_a = over_core(block_a, behind_a, y_a, (0, 2))
    core_2 = over_core(block_a, behind_a, y_a, (2, 1))
    full_a = (block_a, behind_a[0], y_a)
    piece_0 = own(full_a, 0, core_a, 0, 0)
    recv_0 = relay(piece_0[:cut])
    piece_1 = own(gate(full_a, piece_0), 1, core_a, 1, 1)
    piece_2 = own(gate(full_a, piece_1), 2, core_2, 0, 2)
    recv_1 = relay(jnp.concatenate([piece_0[cut:], piece_1, piece_2[:cut]]))
    block_b, block_f = gate((block_b, block_f), behind_f, y_b, recv_0, piece_2, wide_b)
    core_b = [over_core(block_b, behind_b, y_b, (n, 1)) for n in range(chunk_b[1])]
    y_f = over_y(block_f, behind_f, whole(chunk_f))
    full_b = (block_b, behind_b[0], y_b)
    piece_3 = own(full_b, 0, core_b[0], 0, 3)
    piece_4 = own(gate(full_b, piece_3), 1, core_b[1], 0, 4)
    recv_2 = relay(jnp.concatenate([piece_2[cut:], piece_3, piece_4]))
    block_f = gate(block_f, piece_4, recv_1)
    core_f = over_core(block_f, behind_f, y_f, (0, 2))
    rest = tokens - cut
    early = [
        (recv_0, (0, 0)),
        (recv_1[:rest], (cut, 0)),
        (recv_1[rest : rest + tokens], (0, WIDTH)),
        (recv_1[rest + tokens :], (0, 2 * WIDTH)),
    ]
    out = assemble(None, early, queries.shape, LIGHT)
    core_7 = over_core(gate(block_f, out), behind_f, y_f, (2, 1))
    full_f = (block_f, behind_f[0], y_f)
    piece_5 = passed(full_f, 0, core_f, 0, query_5, 0, 0)
    piece_6 = passed(gate(full_f, piece_5), 1, core_f, 1, wide_b, tokens, 2 * tokens)
    piece_7 = passed(gate(full_f, piece_6), 2, core_7, 0, wide_b, 3 * tokens, 4 * tokens)
    recv_2 = gate(recv_2, piece_7)
    late = [
        (piece_5, (0, 5 * WIDTH)),
        (piece_6, (0, 6 * WIDTH)),
        (piece_7, (0, 7 * WIDTH)),
        (recv_2[:rest], (cut, 2 * WIDTH)),
        (recv_2[rest : rest + tokens], (0, 3 * WIDTH)),
        (recv_2[rest + tokens :], (0, 4 * WIDTH)),
    ]
    return assemble(out, late, queries.shape, LIGHT)[None]


def solution(mesh):
    in_specs = (
        P("section", "ctx", None),
        P("section", "ctx", None),
        P("section", "ctx", None),
        P("section", "ctx", None),
        P("section", "ctx"),
    )
    out_specs = P("section", "ctx", None)
    return jax.shard_map(local, mesh=mesh, in_specs=in_specs, out_specs=out_specs, check_vma=False)
```

```python
import functools
import math

import jax
import jax.numpy as jnp
from jax import lax
from jax.experimental import pallas as pl
from jax.experimental.pallas import tpu as pltpu
from jax.sharding import PartitionSpec as P

HQ = 64
KVH = 8
HD = 128
WINDOW = 8
REPEAT = HQ // KVH
PAIR = 2 * HD
WIDTH = REPEAT * HD
SEG_ROWS = 16
PENALTY = float(2**20)
LOG2_SCALE = HD**-0.5 * math.log2(math.e)
LIGHT = pl.CostEstimate(flops=1, bytes_accessed=1, transcendentals=0)
HEAVY = pl.CostEstimate(flops=10**11, bytes_accessed=10**6, transcendentals=0)
SLOTS = (
    (7, 3, 5, 1, 4, 6, 2, 0),
    (7, 3, 5, 1, 2, 4, 0, 6),
    (7, 3, 1, 5, 4, 2, 6, 0),
    (7, 3, 1, 5, 2, 0, 4, 6),
)


def gate(value, *ahead):
    return lax.optimization_barrier((value, ahead))[0]


def exchange(value, axis, bit):
    return lax.ppermute(value, axis, [(i, i ^ bit) for i in range(lax.axis_size(axis))])


def from_groups_behind(value, groups):
    size = lax.axis_size("ctx")
    pairs = [(i, i + 4 * groups) for i in range(size - 4 * groups)]
    if not {a for a, _ in pairs} & {b for _, b in pairs}:
        pairs = pairs + [(b, a) for a, b in pairs]
    return lax.ppermute(value, "ctx", pairs)


def gather_behind(block):
    return from_groups_behind(block, 1), from_groups_behind(block, 2)


def join_kernel(bit, column, *refs):
    *parts, own, two, out = refs
    width = out.shape[1]
    row = 0
    for part in parts:
        start = column if part.shape[1] > width else 0
        out[row : row + part.shape[0], :] = part[:, start : start + width]
        row += part.shape[0]
    first = (lax.axis_index("ctx") // bit) % 2 == 0

    @pl.when(first)
    def _():
        out[row:, :] = own[:, column : column + width]

    @pl.when(jnp.logical_not(first))
    def _():
        out[row:, :] = two[:, column : column + width]


def join(parts, own, two, bit, chunk):
    first, size = chunk
    rows = sum(part.shape[0] for part in parts) + own.shape[0]
    vmem = pl.BlockSpec(memory_space=pltpu.VMEM)
    return pl.pallas_call(
        functools.partial(join_kernel, bit, first * PAIR),
        in_specs=[vmem] * (len(parts) + 2),
        out_specs=vmem,
        out_shape=jax.ShapeDtypeStruct((rows, size * PAIR), jnp.bfloat16),
        cost_estimate=LIGHT,
        compiler_params=pltpu.CompilerParams(vmem_limit_bytes=12 * 2**20),
        name="join",
    )(*parts, own, two)


def over_y(block, behind, chunk):
    one, two = behind
    return exchange(join([one], block, two, 2, chunk), "ctx", 2)


def over_core(block, behind, mates, chunk):
    one, two = behind
    return exchange(join([one, mates], block, two, 1, chunk), "ctx", 1)


def fill_block(out, tokens, chunk, keys, values, seg):
    first, size = chunk
    for n in range(size):
        source = slice((first + n) * HD, (first + n + 1) * HD)
        out[:tokens, n * PAIR : n * PAIR + HD] = keys[:, source]
        out[:tokens, n * PAIR + HD : (n + 1) * PAIR] = values[:, source]
    out[tokens:, :] = jnp.zeros((out.shape[0] - tokens, size * PAIR), jnp.bfloat16)
    row = seg[...].astype(jnp.float32).astype(jnp.bfloat16)
    for n in range(size):
        out[tokens : tokens + 1, n * PAIR : n * PAIR + tokens] = row


def pack_first_kernel(chunks, keys_in, values_in, seg_in, *refs):
    *blocks, keys, values, seg, sems = refs
    copies = [
        pltpu.make_async_copy(source, target, sems.at[n])
        for n, (source, target) in enumerate(
            ((keys_in, keys), (values_in, values), (seg_in, seg))
        )
    ]
    for copy in copies:
        copy.start()
    for copy in copies:
        copy.wait()
    for target, chunk in zip(blocks, chunks):
        fill_block(target, keys.shape[0], chunk, keys, values, seg)


def pack_first(keys, values, segments, chunks):
    shapes = [(keys.shape[0] + SEG_ROWS, size * PAIR) for _, size in chunks]
    vmem = pl.BlockSpec(memory_space=pltpu.VMEM)
    return pl.pallas_call(
        functools.partial(pack_first_kernel, chunks),
        in_specs=[pl.BlockSpec(memory_space=pltpu.HBM)] * 3,
        out_specs=[vmem] * len(shapes),
        out_shape=[jax.ShapeDtypeStruct(shape, jnp.bfloat16) for shape in shapes],
        scratch_shapes=[
            pltpu.VMEM(keys.shape, jnp.bfloat16),
            pltpu.VMEM(values.shape, jnp.bfloat16),
            pltpu.VMEM(segments.shape, segments.dtype),
            pltpu.SemaphoreType.DMA((3,)),
        ],
        cost_estimate=LIGHT,
        compiler_params=pltpu.CompilerParams(vmem_limit_bytes=56 * 2**20),
        name="pack_first",
    )(keys, values, segments)


def pack_wide_kernel(parts, queries, stream, out, sems):
    tokens = queries.shape[0]
    copies = [
        pltpu.make_async_copy(
            (queries, stream)[m].at[:, pl.ds(head * WIDTH, WIDTH)],
            out.at[pl.ds(n * tokens, tokens)],
            sems.at[n],
        )
        for n, (m, head) in enumerate(parts)
    ]
    for copy in copies:
        copy.start()
    for copy in copies:
        copy.wait()


def pack_wide(queries, stream, parts):
    return pl.pallas_call(
        functools.partial(pack_wide_kernel, parts),
        in_specs=[pl.BlockSpec(memory_space=pltpu.HBM)] * 2,
        out_specs=pl.BlockSpec(memory_space=pltpu.VMEM),
        out_shape=jax.ShapeDtypeStruct((len(parts) * queries.shape[0], WIDTH), jnp.bfloat16),
        scratch_shapes=[pltpu.SemaphoreType.DMA((len(parts),))],
        cost_estimate=LIGHT,
        compiler_params=pltpu.CompilerParams(vmem_limit_bytes=56 * 2**20),
        name="pack_wide",
    )(queries, stream)


def attend_kernel(tokens, column, query_row, stream_row, *refs):
    blocks, (query_in, stream_in, out) = refs[:WINDOW], refs[WINDOW : WINDOW + 3]
    keys, values, bias, extra, segs_ref, query, stream, sems = refs[WINDOW + 3 :]
    window = tokens * WINDOW
    index = lax.axis_index("ctx")
    place = index % 4
    slots = [
        jnp.where(place < 2, jnp.where(place == 0, a, b), jnp.where(place == 2, c, d))
        for a, b, c, d in zip(*SLOTS)
    ]
    copies = [
        pltpu.make_async_copy(
            source.at[pl.ds(row, tokens), pl.ds(column, WIDTH)], target, sems.at[n]
        )
        for n, (source, row, target) in enumerate(
            ((query_in, query_row, query), (stream_in, stream_row, stream))
        )
    ]

    for copy in copies:
        copy.start()
    for slot, block in zip(slots, blocks):
        row = block[tokens : tokens + 1, :].astype(jnp.float32)
        segs_ref[pl.ds(slot, 1), :] = jnp.where(slot + index >= WINDOW - 1, row, -1.0)
    segs = segs_ref[...]
    own_row = segs[WINDOW - 1 :, :tokens]
    seg_zero = segs[WINDOW - 1 :, 0:1]
    own_column = segs.T[:tokens, WINDOW - 1 :]
    before = jnp.sum(jnp.where(segs[: WINDOW - 1, :tokens] != seg_zero, 1.0, 0.0))
    lane = lax.broadcasted_iota(jnp.int32, (tokens, HD), 1)
    extra[...] = jnp.where(
        lane == 0,
        jnp.where(own_column == seg_zero, 0.0, -PENALTY),
        jnp.where(lane == 1, -PENALTY, 0.0),
    ).astype(jnp.bfloat16)
    row_id = lax.broadcasted_iota(jnp.int32, (tokens, tokens), 0)
    column_id = lax.broadcasted_iota(jnp.int32, (tokens, tokens), 1)
    tail = bias.shape[1]
    bias[:, : tail - tokens] = jnp.zeros((tokens, tail - tokens), jnp.float32)
    bias[:, tail - tokens :] = jnp.where(
        (own_column == own_row) & (column_id <= row_id), 0.0, -PENALTY
    )
    key_row = lax.broadcasted_iota(jnp.int32, (window, HD), 0)
    key_lane = lax.broadcasted_iota(jnp.int32, (window, HD), 1)
    keys[:, HD:] = jnp.where(
        ((key_lane == 0) & (key_row < window - tokens))
        | ((key_lane == 1) & (key_row.astype(jnp.float32) < before)),
        1.0,
        0.0,
    ).astype(jnp.bfloat16)
    values[:, HD:] = jnp.ones((window, HD), jnp.bfloat16)

    for copy in copies:
        copy.wait()

    for slot, block in zip(slots, blocks):
        rows = pl.ds(pl.multiple_of(slot * tokens, tokens), tokens)
        keys[rows, :HD] = block[:tokens, :HD]
        values[rows, :HD] = block[:tokens, HD:]

    def columns(head):
        return slice(head * HD, (head + 1) * HD)

    def score(head):
        marks = extra[...]
        rows = jnp.concatenate(
            [jnp.concatenate([query[:, columns(h)], marks], axis=1) for h in (head, head + 1)],
            axis=0,
        )
        scores = lax.dot_general(
            rows, keys[...], (((1,), (1,)), ((), ())), preferred_element_type=jnp.float32
        )
        own = scores[:, window - tail :] + jnp.concatenate([bias[...]] * 2, axis=0)
        return jnp.concatenate([scores[:, : window - tail], own], axis=1)

    def finish(head, scores):
        top = jnp.max(scores, axis=1, keepdims=True)
        weights = jnp.exp2((scores - top) * LOG2_SCALE).astype(jnp.bfloat16)
        sums = jnp.dot(weights, values[...], preferred_element_type=jnp.float32)
        attended = sums[:, :HD] / sums[:, HD:]
        for n, h in enumerate((head, head + 1)):
            out[:, columns(h)] = (
                attended[n * tokens : (n + 1) * tokens]
                + stream[:, columns(h)].astype(jnp.float32)
            ).astype(jnp.bfloat16)

    scores = score(0)
    for head in range(0, REPEAT, 2):
        later = score(head + 2) if head + 2 < REPEAT else None
        finish(head, scores)
        scores = later


def attend(blocks, queries, stream, column, query_row, stream_row, cost):
    rows = blocks[0][0].shape[0]
    tokens = rows - SEG_ROWS
    window = tokens * WINDOW
    places = [(block, part, n) for block, part in blocks for n in range(block.shape[0] // rows)]
    return pl.pallas_call(
        functools.partial(attend_kernel, tokens, column, query_row, stream_row),
        grid=(1,),
        in_specs=[
            pl.BlockSpec((rows, PAIR), lambda i, part=part, n=n: (n, part)) for _, part, n in places
        ]
        + [pl.BlockSpec(memory_space=pl.ANY)] * 2,
        out_specs=pl.BlockSpec((tokens, WIDTH), lambda i: (0, 0)),
        out_shape=jax.ShapeDtypeStruct((tokens, WIDTH), jnp.bfloat16),
        scratch_shapes=[
            pltpu.VMEM((window, PAIR), jnp.bfloat16),
            pltpu.VMEM((window, PAIR), jnp.bfloat16),
            pltpu.VMEM((tokens, PAIR), jnp.float32),
            pltpu.VMEM((tokens, HD), jnp.bfloat16),
            pltpu.VMEM((WINDOW, PAIR), jnp.float32),
            pltpu.VMEM((tokens, WIDTH), jnp.bfloat16),
            pltpu.VMEM((tokens, WIDTH), jnp.bfloat16),
            pltpu.SemaphoreType.DMA((2,)),
        ],
        compiler_params=pltpu.CompilerParams(vmem_limit_bytes=16 * 2**20),
        cost_estimate=cost,
        name="attend",
    )(*[block for block, _, _ in places], queries, stream)


def assemble_kernel(places, *refs):
    *pieces, out, sems = refs
    copies = [
        pltpu.make_async_copy(
            piece, out.at[pl.ds(row, piece.shape[0]), pl.ds(column, piece.shape[1])], sems.at[n]
        )
        for n, (piece, (row, column)) in enumerate(zip(pieces[-len(places) :], places))
    ]
    for copy in copies:
        copy.start()
    for copy in copies:
        copy.wait()


def assemble(out, pieces, shape, cost):
    places = [place for _, place in pieces]
    given = [] if out is None else [out]
    return pl.pallas_call(
        functools.partial(assemble_kernel, places),
        in_specs=[pl.BlockSpec(memory_space=pl.ANY)] * len(given)
        + [pl.BlockSpec(memory_space=pltpu.VMEM)] * len(pieces),
        out_specs=pl.BlockSpec(memory_space=pl.ANY),
        out_shape=jax.ShapeDtypeStruct(shape, jnp.bfloat16),
        scratch_shapes=[pltpu.SemaphoreType.DMA((len(pieces),))],
        input_output_aliases={0: 0} if given else {},
        cost_estimate=cost,
        compiler_params=pltpu.CompilerParams(vmem_limit_bytes=8 * 2**20),
        name="assemble",
    )(*given, *[piece for piece, _ in pieces])


def local(stream, queries, keys, values, segments):
    stream, queries, keys, values = stream[0], queries[0], keys[0], values[0]
    segments = segments.reshape(1, -1)
    tokens = queries.shape[0]
    relay = lambda value: exchange(value, "section", 1)
    def own(full, n, core, at, head):
        at = [(part, n) for part in full] + [(core, at)]
        return attend(at, queries, stream, head * WIDTH, 0, 0, LIGHT)

    def passed(full, n, core, at, q, q_row, s_row):
        at = [(part, n) for part in full] + [(core, at)]
        return attend(at, q, wide_b, 0, q_row, s_row, LIGHT)

    chunk_a, chunk_b, chunk_f = (0, 3), (3, 2), (5, 3)
    cut = 3 * tokens // 4
    whole = lambda chunk: (0, chunk[1])
    query_5 = queries[:, 5 * WIDTH : 6 * WIDTH]
    keys = gate(keys, query_5)
    query_5 = relay(query_5)
    block_a, block_b, block_f = pack_first(keys, values, segments, (chunk_a, chunk_b, chunk_f))
    block_f = relay(block_f)
    behind_a = gather_behind(block_a)
    wide_b = pack_wide(gate(queries, block_a), stream, ((1, 5), (0, 6), (1, 6), (0, 7), (1, 7)))
    wide_b, behind_a = relay(wide_b), gate(behind_a, block_f, query_5)
    behind_b = gather_behind(gate(block_b, behind_a))
    y_a = over_y(block_a, behind_a, whole(chunk_a))
    behind_f = gather_behind(gate(block_f, behind_b, y_a))
    y_b = over_y(gate(block_b, y_a), behind_b, whole(chunk_b))
    block_a = gate(block_a, behind_b)
    core_a = over_core(block_a, behind_a, y_a, (0, 2))
    core_2 = over_core(block_a, behind_a, y_a, (2, 1))
    full_a = (block_a, behind_a[0], y_a)
    piece_0 = own(full_a, 0, core_a, 0, 0)
    recv_0 = relay(piece_0[:cut])
    piece_1 = own(gate(full_a, piece_0), 1, core_a, 1, 1)
    piece_2 = own(gate(full_a, piece_1), 2, core_2, 0, 2)
    recv_1 = relay(jnp.concatenate([piece_0[cut:], piece_1, piece_2[:cut]]))
    block_b, block_f = gate((block_b, block_f), behind_f, y_b, recv_0, piece_2, wide_b)
    core_b = [over_core(block_b, behind_b, y_b, (n, 1)) for n in range(chunk_b[1])]
    y_f = over_y(block_f, behind_f, whole(chunk_f))
    full_b = (block_b, behind_b[0], y_b)
    piece_3 = own(full_b, 0, core_b[0], 0, 3)
    piece_4 = own(gate(full_b, piece_3), 1, core_b[1], 0, 4)
    recv_2 = relay(jnp.concatenate([piece_2[cut:], piece_3, piece_4]))
    block_f = gate(block_f, piece_4, recv_1)
    core_f = over_core(block_f, behind_f, y_f, (0, 2))
    rest = tokens - cut
    early = [
        (recv_0, (0, 0)),
        (recv_1[:rest], (cut, 0)),
        (recv_1[rest : rest + tokens], (0, WIDTH)),
        (recv_1[rest + tokens :], (0, 2 * WIDTH)),
    ]
    out = assemble(None, early, queries.shape, LIGHT)
    core_7 = over_core(gate(block_f, out), behind_f, y_f, (2, 1))
    full_f = (block_f, behind_f[0], y_f)
    piece_5 = passed(full_f, 0, core_f, 0, query_5, 0, 0)
    piece_6 = passed(gate(full_f, piece_5), 1, core_f, 1, wide_b, tokens, 2 * tokens)
    piece_7 = passed(gate(full_f, piece_6), 2, core_7, 0, wide_b, 3 * tokens, 4 * tokens)
    late = [
        (piece_5, (0, 5 * WIDTH)),
        (piece_6, (0, 6 * WIDTH)),
        (piece_7, (0, 7 * WIDTH)),
    ]
    out = assemble(out, late, queries.shape, LIGHT)
    recv_2 = gate(recv_2, out)
    last = [
        (recv_2[:rest], (cut, 2 * WIDTH)),
        (recv_2[rest : rest + tokens], (0, 3 * WIDTH)),
        (recv_2[rest + tokens :], (0, 4 * WIDTH)),
    ]
    return assemble(out, last, queries.shape, LIGHT)[None]


def solution(mesh):
    in_specs = (
        P("section", "ctx", None),
        P("section", "ctx", None),
        P("section", "ctx", None),
        P("section", "ctx", None),
        P("section", "ctx"),
    )
    out_specs = P("section", "ctx", None)
    return jax.shard_map(local, mesh=mesh, in_specs=in_specs, out_specs=out_specs, check_vma=False)
```
